128 devices in a mesh: ctx: 32 (over z, x, core), wsh: 4 (over y).
Axes of the slice: x: 4, y: 4, z: 4, core: 2. Of those that a mesh axis runs over, the one named last changes fastest.
Arguments:
- tokens: bfloat16 [4, 4096, 960], P('wsh', 'ctx'), may hold values from -6 to 6
- cotangent: bfloat16 [4, 4096, 960], P('wsh', 'ctx'), may hold values from -6 to 6
- blocks: int32 [64], replicated, may hold values from 0 to 63, as said below
- attend_weight: float32 [960, 1600], P('wsh', 'ctx'), may hold values from -0.1875 to 0.1875
- output_weight: float32 [960, 960], P('wsh', 'ctx'), may hold values from -2 to 2
- gateup_weight: float32 [960, 5120], P('wsh', 'ctx'), may hold values from -0.1875 to 0.1875
- down_weight: float32 [2560, 960], P('wsh', 'ctx'), may hold values from -0.125 to 0.125
- norm_gains: float32 [2, 960], P(None, 'ctx'), may hold values from 0.5 to 1.5
- attend_first: float32 [960, 1600], P('wsh', 'ctx'), may hold values from -40 to 40
- output_first: float32 [960, 960], P('wsh', 'ctx'), may hold values from -6 to 6
- gateup_first: float32 [960, 5120], P('wsh', 'ctx'), may hold values from -24 to 24
- down_first: float32 [2560, 960], P('wsh', 'ctx'), may hold values from -40 to 40
- gains_first: float32 [2, 960], P(None, 'ctx'), may hold values from -80 to 80
- attend_second: float32 [960, 1600], P('wsh', 'ctx'), may hold values from 216.2688 to 861.7984
- output_second: float32 [960, 960], P('wsh', 'ctx'), may hold values from 8.6 to 34.4
- gateup_second: float32 [960, 5120], P('wsh', 'ctx'), may hold values from 77.49632 to 309.6576
- down_second: float32 [2560, 960], P('wsh', 'ctx'), may hold values from 216.2688 to 861.7984
- gains_second: float32 [2, 960], P(None, 'ctx'), may hold values from 861.7984 to 3440.64
Outputs:
- layer_output: bfloat16 [4, 4096, 960], P('wsh', 'ctx')
- input_grad: float32 [4, 4096, 960], P('wsh', 'ctx')
- next_attend: float32 [960, 1600], P('wsh', 'ctx')
- next_attend_first: float32 [960, 1600], P('wsh', 'ctx')
- next_attend_second: float32 [960, 1600], P('wsh', 'ctx')
- next_output: float32 [960, 960], P('wsh', 'ctx')
- next_output_first: float32 [960, 960], P('wsh', 'ctx')
- next_output_second: float32 [960, 960], P('wsh', 'ctx')
- next_gateup: float32 [960, 5120], P('wsh', 'ctx')
- next_gateup_first: float32 [960, 5120], P('wsh', 'ctx')
- next_gateup_second: float32 [960, 5120], P('wsh', 'ctx')
- next_down: float32 [2560, 960], P('wsh', 'ctx')
- next_down_first: float32 [2560, 960], P('wsh', 'ctx')
- next_down_second: float32 [2560, 960], P('wsh', 'ctx')
- next_gains: float32 [2, 960], P(None, 'ctx')
- next_gains_first: float32 [2, 960], P(None, 'ctx')
- next_gains_second: float32 [2, 960], P(None, 'ctx')
The draws below stay inside these ranges and needn't reach their ends.
Inputs may be any that keep to these rules, and one draw needn't show every extreme that they name: Entries 2i and 2i+1 are the causal blocks of the i-th group of 128 rows: one block b and its mirror 64 - 1 - b, in either order; every block appears once.
All inputs are finite; a program needn't handle non-finite values.
Results may differ from the reference program's by a relative error of at most 0.035.
Values may be sent and summed in bfloat16 or wider, within the bound.
No kernel may reach another device: no remote copies, remote signals or barrier semaphores. Data moves between devices by JAX's collectives and lax.ppermute only.
A program may use at most 128 MiB of HBM per device.

```python
import math
import jax
import jax.numpy as jnp
from jax import lax

D = 960
QUERY_HEADS = 15
KEY_VALUE_HEADS = 5
HEAD_DIMENSION = 64
FF = 2560
STEP = 5
BLK = 64
NBLOCKS = 64
LENGTH = 4096
SEQS = 4
ALL_TOKENS = 16384
QKV = 1600


def draw_blocks(key, part):
    key = jax.random.fold_in(key, 7)
    order_key, flip_key = jax.random.split(key)
    order_perm = jax.random.permutation(order_key, NBLOCKS // 2)
    flip_bits = jax.random.randint(flip_key, (NBLOCKS // 2,), 0, 2)
    mirror = NBLOCKS - 1 - order_perm
    front_block = jnp.where(flip_bits == 1, mirror, order_perm)
    back_block = jnp.where(flip_bits == 1, order_perm, mirror)
    return jnp.stack([front_block, back_block], axis=1).reshape(NBLOCKS).astype(jnp.int32)


def block_scale(stream_key, dims, shards, smallest, largest):
    factor_of = 1.0
    for dim, blocks in shards:
        heights = jax.random.uniform(jax.random.fold_in(jax.random.fold_in(stream_key, 6), dim), (blocks,), jnp.float32, smallest / len(shards), largest / len(shards))
        factor_of = factor_of * jnp.repeat(jnp.exp(heights), dims[dim] // blocks).reshape((-1,) + (1,) * (len(dims) - 1 - dim))
    return factor_of


def gaussian(rng, dims, scale, bound, cuts=(), kind=jnp.bfloat16):
    level = block_scale(rng, dims, cuts, -0.22, 0.18) if cuts else 1.0
    entries = jax.random.normal(rng, dims, jnp.float32) * scale * level
    return jnp.minimum(jnp.maximum(entries, -bound), bound).astype(kind)


def setup_inputs(seed: int = 0) -> dict:
    key_list = jax.random.split(jax.random.key(seed), 19)
    return {
        "tokens": gaussian(key_list[0], (SEQS, LENGTH, D), 1.0, 6.0, ((0, 4), (1, 32))),
        "cotangent": gaussian(key_list[1], (SEQS, LENGTH, D), 1.0, 6.0, ((0, 4), (1, 32))),
        "blocks": draw_blocks(jax.random.fold_in(key_list[18], 71), 0),
        "attend_weight": gaussian(key_list[3], (D, QKV), D ** -0.5, 0.1875, ((0, 4), (1, 32)), jnp.float32),
        "output_weight": gaussian(key_list[4], (QUERY_HEADS * HEAD_DIMENSION, D), (max(1, QUERY_HEADS * HEAD_DIMENSION * 32 // LENGTH)) ** -0.5, 2.0, ((0, 4), (1, 32)), jnp.float32),
        "gateup_weight": gaussian(key_list[5], (D, 2 * FF), D ** -0.5, 0.1875, ((0, 4), (1, 32)), jnp.float32),
        "down_weight": gaussian(key_list[6], (FF, D), FF ** -0.5, 0.125, ((0, 4), (1, 32)), jnp.float32),
        "norm_gains": jnp.clip(1.0 + 0.1 * jax.random.normal(key_list[7], (2, D), jnp.float32), 0.5, 1.5),
        "attend_first": gaussian(key_list[8], (D, QKV), (0.055 * ALL_TOKENS ** 0.5), 40.0, ((0, 4), (1, 32)), jnp.float32),
        "output_first": gaussian(key_list[9], (QUERY_HEADS * HEAD_DIMENSION, D), (0.7 * SEQS ** 0.5), 6.0, ((0, 4), (1, 32)), jnp.float32),
        "gateup_first": gaussian(key_list[10], (D, 2 * FF), (0.033 * ALL_TOKENS ** 0.5), 24.0, ((0, 4), (1, 32)), jnp.float32),
        "down_first": gaussian(key_list[11], (FF, D), (0.055 * ALL_TOKENS ** 0.5), 40.0, ((0, 4), (1, 32)), jnp.float32),
        "gains_first": gaussian(key_list[12], (2, D), (0.11 * ALL_TOKENS ** 0.5), 80.0, ((1, 32),), jnp.float32),
        "attend_second": jnp.clip(jnp.exp(math.log(861.7984) - 1.3824993 * jax.random.uniform(key_list[13], (D, QKV), jnp.float32) ** block_scale(key_list[13], (D, QKV), ((0, 4), (1, 32)), -0.2, 0.2)), 216.2688, 861.7984),
        "output_second": jnp.clip(jnp.exp(math.log(34.4) - 1.3862944 * jax.random.uniform(key_list[14], (QUERY_HEADS * HEAD_DIMENSION, D), jnp.float32) ** block_scale(key_list[14], (QUERY_HEADS * HEAD_DIMENSION, D), ((0, 4), (1, 32)), -0.2, 0.2)), 8.6, 34.4),
        "gateup_second": jnp.clip(jnp.exp(math.log(309.6576) - 1.38523666 * jax.random.uniform(key_list[15], (D, 2 * FF), jnp.float32) ** block_scale(key_list[15], (D, 2 * FF), ((0, 4), (1, 32)), -0.2, 0.2)), 77.49632, 309.6576),
        "down_second": jnp.clip(jnp.exp(math.log(861.7984) - 1.3824993 * jax.random.uniform(key_list[16], (FF, D), jnp.float32) ** block_scale(key_list[16], (FF, D), ((0, 4), (1, 32)), -0.2, 0.2)), 216.2688, 861.7984),
        "gains_second": jnp.clip(jnp.exp(math.log(3440.64) - 1.3843914 * jax.random.uniform(key_list[17], (2, D), jnp.float32) ** block_scale(key_list[17], (2, D), ((1, 32),), -0.2, 0.2)), 861.7984, 3440.64),
    }


@jax.custom_vjp
def lower_precision(v):
    return lax.optimization_barrier(v.astype(jnp.bfloat16)).astype(jnp.float32)

@jax.custom_vjp
def low_back(v):
    return v

def low_keep(v):
    return (lower_precision(v), None)

def low_pass(kept, grad):
    return (grad,)

def back_keep(v):
    return (v, None)

def back_low(kept, grad):
    return (lower_precision(grad),)
lower_precision.defvjp(low_keep, low_pass)
low_back.defvjp(back_keep, back_low)
beta_one = 0.9
beta_two = 0.95
adam_eps = 1e-08
norm_eps = 1e-05

def matmul(left, right):
    return jnp.dot(left, right, precision=lax.Precision.HIGHEST)

def rotary_tables(positions, head_size):
    half_size = head_size // 2
    inverse = jnp.power(10000.0, -2.0 * jnp.arange(half_size, dtype=jnp.float32) / head_size)
    angles = positions.astype(jnp.float32)[:, None] * inverse[None, :]
    return (jnp.cos(angles), jnp.sin(angles))

def apply_rotation(value_rows, cosine_table, sine_table, heads, head_size, direction):
    shaped = value_rows.reshape(value_rows.shape[0], heads, head_size)
    half_size = head_size // 2
    front_half = shaped[..., :half_size]
    back_half = shaped[..., half_size:]
    cosine_rows = cosine_table[:, None, :]
    sine_rows = direction * sine_table[:, None, :]
    rotated = jnp.concatenate([front_half * cosine_rows - back_half * sine_rows, back_half * cosine_rows + front_half * sine_rows], axis=-1)
    return rotated.reshape(value_rows.shape)

def normalize(value_rows, gain):
    inverse_rms = lax.rsqrt(lax.optimization_barrier(jnp.mean(value_rows * value_rows, axis=-1, keepdims=True)) + norm_eps)
    return value_rows * inverse_rms * gain

def attention(query_matrix, key_rows, value_rows, positions):
    sequence_length = query_matrix.shape[0]
    group_size = QUERY_HEADS // KEY_VALUE_HEADS
    width_of_block = math.gcd(sequence_length, 512)
    blocks_of_query = query_matrix.reshape(sequence_length // width_of_block, width_of_block, KEY_VALUE_HEADS, group_size, HEAD_DIMENSION)
    position_blocks = positions.reshape(sequence_length // width_of_block, width_of_block)
    heads_of_key = key_rows.reshape(sequence_length, KEY_VALUE_HEADS, HEAD_DIMENSION)
    heads_of_value = value_rows.reshape(sequence_length, KEY_VALUE_HEADS, HEAD_DIMENSION)
    score_scale = HEAD_DIMENSION ** (-0.5)

    def one_block(block_item):
        query_rows, query_pos = block_item
        scores = jnp.einsum('qhgd,khd->hgqk', query_rows, heads_of_key, precision=lax.Precision.HIGHEST) * score_scale
        allowed = positions[None, :] <= query_pos[:, None]
        scores = low_back(jnp.where(allowed, scores, -1e+30))
        peak = lax.optimization_barrier(jnp.max(scores, axis=-1, keepdims=True))
        exps = jnp.exp(scores - peak)
        chances = lower_precision(exps / lax.optimization_barrier(jnp.sum(exps, axis=-1, keepdims=True)))
        result = jnp.einsum('hgqk,khd->qhgd', chances, heads_of_value, precision=lax.Precision.HIGHEST)
        return result.reshape(width_of_block, QUERY_HEADS * HEAD_DIMENSION)
    outputs = lax.map(jax.checkpoint(one_block), (blocks_of_query, position_blocks))
    return outputs.reshape(sequence_length, QUERY_HEADS * HEAD_DIMENSION)

def layer(inputs, params, positions):
    attend_weight, output_weight, gateup_weight, down_weight, norm_gains = params
    attend_low = lower_precision(attend_weight)
    output_low = lower_precision(output_weight)
    gateup_low = lower_precision(gateup_weight)
    down_low = lower_precision(down_weight)
    gains_low = lower_precision(norm_gains)
    query_columns = QUERY_HEADS * HEAD_DIMENSION
    key_columns = KEY_VALUE_HEADS * HEAD_DIMENSION
    first_norm = lower_precision(normalize(inputs, gains_low[0]))
    mixed_heads = low_back(matmul(first_norm, attend_low))
    cosine_table, sine_table = rotary_tables(positions, HEAD_DIMENSION)
    query_matrix = lower_precision(apply_rotation(mixed_heads[:, :query_columns], cosine_table, sine_table, QUERY_HEADS, HEAD_DIMENSION, 1.0))
    key_rows = lower_precision(apply_rotation(mixed_heads[:, query_columns:query_columns + key_columns], cosine_table, sine_table, KEY_VALUE_HEADS, HEAD_DIMENSION, 1.0))
    value_rows = lower_precision(mixed_heads[:, query_columns + key_columns:])
    attended = low_back(lower_precision(attention(query_matrix, key_rows, value_rows, positions)))
    middle = inputs + low_back(matmul(attended, output_low))
    second_norm = lower_precision(normalize(middle, gains_low[1]))
    gate_up = low_back(matmul(second_norm, gateup_low))
    gate_part = gate_up[:, :FF]
    up_part = gate_up[:, FF:]
    hidden = lower_precision(gate_part * jax.nn.sigmoid(gate_part) * up_part)
    return middle + low_back(matmul(hidden, down_low))

def adamw(weight, first_old, second_old, gradient, rate, decay):
    first_next = beta_one * first_old + (1.0 - beta_one) * gradient
    second_next = beta_two * second_old + (1.0 - beta_two) * gradient * gradient
    first_hat = first_next / (1.0 - beta_one ** STEP)
    second_hat = second_next / (1.0 - beta_two ** STEP)
    weight_next = weight - rate * (first_hat / (jnp.sqrt(second_hat) + adam_eps) + decay * weight)
    return (weight_next, first_next, second_next)

def reference(tokens, cotangent, blocks, attend_weight, output_weight, gateup_weight, down_weight, norm_gains, attend_first, output_first, gateup_first, down_first, gains_first, attend_second, output_second, gateup_second, down_second, gains_second):
    offsets = jnp.arange(BLK, dtype=jnp.int32)
    positions = (blocks[:, None] * BLK + offsets[None, :]).reshape(LENGTH).astype(jnp.int32)
    params = (attend_weight, output_weight, gateup_weight, down_weight, norm_gains)

    def one_sequence(grad_total, seq_item):
        seq_in, seq_back = seq_item

        def run(inputs, weights):
            return layer(inputs, weights, positions)
        result, pull = jax.vjp(run, seq_in.astype(jnp.float32), params)
        in_grad, grads = pull(seq_back.astype(jnp.float32))
        grad_total = jax.tree.map(jnp.add, grad_total, grads)
        return (grad_total, (result.astype(jnp.bfloat16), in_grad))
    zero_filled = jax.tree.map(jnp.zeros_like, params)
    grads, (layer_output, input_grad) = lax.scan(one_sequence, zero_filled, (tokens, cotangent))
    output_rate = max(1, QUERY_HEADS * HEAD_DIMENSION * 32 // LENGTH) ** (-0.5)
    attend_next = adamw(attend_weight, attend_first, attend_second, grads[0], 0.02, 0.1)
    output_next = adamw(output_weight, output_first, output_second, grads[1], output_rate, 0.1)
    gateup_next = adamw(gateup_weight, gateup_first, gateup_second, grads[2], 0.02, 0.1)
    down_next = adamw(down_weight, down_first, down_second, grads[3], 0.02, 0.1)
    gains_next = adamw(norm_gains, gains_first, gains_second, grads[4], 0.7, 0.0)
    return (layer_output, input_grad, attend_next[0], attend_next[1], attend_next[2], output_next[0], output_next[1], output_next[2], gateup_next[0], gateup_next[1], gateup_next[2], down_next[0], down_next[1], down_next[2], gains_next[0], gains_next[1], gains_next[2])
```

```python
import numpy as np
import jax
import jax.numpy as jnp
from jax import lax
from jax.experimental import pallas as pl
from jax.experimental.pallas import tpu as pltpu
from jax.sharding import PartitionSpec as P

QUERY_HEADS = 15
KEY_VALUE_HEADS = 5
HEAD_DIMENSION = 64
GROUP = 3
BLOCK = 64
CHUNK_BLOCKS = 4
CHUNK = BLOCK * CHUNK_BLOCKS
HALF_WIDTH = GROUP * BLOCK
WIDTH = 2 * HALF_WIDTH
NEGATIVE = -1e30
FF = 2560
STEP = 5
ROWS = 128
WIDE = 1024
FEATURES = 960
KV_WIDE = 640
SPLIT = 3
QKV = 1600
CTX = 32
CHIPS = 16
OWN_FF = FF // 2
TILE_FF = 256
UNIT = 160
GRAD_ROWS = 240
GRAD_CUT = 128
REST_CUT = 144
NT = (((1,), (1,)), ((), ()))
TN = (((0,), (0,)), ((), ()))
NN = (((1,), (0,)), ((), ()))

beta_one = 0.9
beta_two = 0.95
adam_eps = 1e-08
norm_eps = 1e-05


def place(index):
    return index // 8, index // 2 % 4, index % 2


def index_of(z, x, core):
    return (z * 4 + x) * 2 + core


def neighbour(value, pairing):
    if pairing == 0:
        return value ^ 1
    return (value + 1) % 4 if value % 2 else (value - 1) % 4


def partner_list(axis, step):
    partners = []
    for index in range(CTX):
        z, x, core = place(index)
        pairing = step ^ core
        if axis == "z":
            partners.append(index_of(neighbour(z, pairing), x, core))
        else:
            partners.append(index_of(z, neighbour(x, pairing), core))
    return partners


PLANS = (
    [partner_list("x", 0), partner_list("x", 1), partner_list("z", 0), partner_list("z", 1)],
    [partner_list("z", 0), partner_list("z", 1), partner_list("x", 0), partner_list("x", 1)],
)
SIBLING = [index ^ 1 for index in range(CTX)]


def origins(plan):
    held = [[index] for index in range(CTX)]
    for partners in plan:
        held = [held[index] + held[partners[index]] for index in range(CTX)]
    held = [held[index] + held[SIBLING[index]] for index in range(CTX)]
    return np.array(held, np.int32)


ORIGINS = [origins(plan) for plan in PLANS]
CHIP_ORDER = np.concatenate(
    [
        ORIGINS[0][:, :CHIPS] // 2,
        ORIGINS[1][:, :CHIPS] // 2,
        ORIGINS[1][SIBLING, :CHIPS] // 2,
        np.argsort(ORIGINS[1][:, :CHIPS] // 2, axis=1),
    ],
    axis=1,
).astype(np.int32)


def swap(value, partners):
    return lax.ppermute(value, "ctx", [(source, target) for source, target in enumerate(partners)])


def after(value, *others):
    return lax.optimization_barrier((value, *others))[0]


def swap_all(values, step):
    return [swap(value, plan[step]) for value, plan in zip(values, PLANS)]


def join(values, got):
    return [jnp.concatenate([value, more], axis=0) for value, more in zip(values, got)]


def core_swap(values, got):
    return [(value, more, swap(value, SIBLING), swap(more, SIBLING)) for value, more in zip(values, got)]


def gather_chips(parts):
    values = [part[None] for part in parts]
    for step in range(3):
        values = join(values, lax.optimization_barrier(swap_all(values, step)))
    return core_swap(values, swap_all(values, 3))


def gather_both(parts, rest):
    values, others = [part[None] for part in parts], [part[None] for part in rest]
    values = join(values, lax.optimization_barrier(swap_all(values, 0)))
    for step in (1, 2):
        got, more = lax.optimization_barrier((swap_all(values, step), swap_all(others, step - 1)))
        values, others = join(values, got), join(others, more)
    got, more = swap_all(values, 3), swap_all(others, 2)
    others = join(others, more)
    return core_swap(values, got), [(other, more) for other, more in zip(others, swap_all(others, 3))]


def add(left, right):
    return (left.astype(jnp.float32) + right.astype(jnp.float32)).astype(jnp.bfloat16)


def scatter_core(parts):
    state = []
    for (low, high, other_low, other_high), plan in zip(parts, PLANS):
        got_high, got_low = swap(other_high, SIBLING), swap(other_low, SIBLING)
        state.append((add(low, got_low), swap(add(high, got_high), plan[3])))
    return state


def scatter_step(state, step):
    following = []
    for (kept, got), plan in zip(state, PLANS):
        half = kept.shape[0] // 2
        more = swap(add(kept[half:], got[half:]), plan[step])
        following.append((add(kept[:half], got[:half]), more))
    return following


def scatter_chips(parts, beside=((), (), ()), rest=()):
    state = scatter_core(parts)
    for step in reversed(range(3)):
        state, rest = lax.optimization_barrier((state, rest, beside[2 - step]))[:2]
        state, rest = scatter_step(state, step), scatter_step(rest, step) if rest else rest
    return [add(kept, got)[0] for kept, got in [*state, *rest]]


def row_partners(step):
    return [neighbour(index % 4, step ^ (index // 4 % 2)) for index in range(4 * CTX)]


def swap_rows(value, step):
    pairs = [(index, index // 4 * 4 + target) for index, target in enumerate(row_partners(step))]
    return lax.ppermute(value, ("ctx", "wsh"), pairs)


def row_order(core, wsh):
    first, second = neighbour(wsh, core), neighbour(wsh, 1 - core)
    return [wsh, first, second, neighbour(second, core)]


ROW_ORDER = np.array([[row_order(core, wsh) for wsh in range(4)] for core in range(2)], np.int32)


def gather_rows(value, wsh_index):
    for bit in (1, 2):
        more = lax.ppermute(value, "wsh", [(source, source ^ bit) for source in range(4)])
        upper = (wsh_index & bit) != 0
        value = jnp.concatenate([jnp.where(upper, more, value), jnp.where(upper, value, more)], axis=1)
    return value


def scatter_rows(value, wsh_index, shared=None):
    pieces = []
    for step in range(4):
        start = (wsh_index + step) % 4 * 256
        piece = lax.dynamic_slice_in_dim(value, start, 256, axis=1)
        if shared is not None:
            piece = jnp.where(shared, value[:, :256], piece)
        if step:
            piece = lax.ppermute(piece, "wsh", [(source, (source + step) % 4) for source in range(4)])
        pieces.append(piece)
    return pieces


def matmul(left, right, dims):
    return lax.dot_general(left, right, dims, preferred_element_type=jnp.float32)


VMEM = pl.BlockSpec(memory_space=pltpu.VMEM)
SMEM = pl.BlockSpec(memory_space=pltpu.SMEM)


def call(kernel, name, out, scratch, args, smem=0, flops=0, moved=0, mib=40):
    return pl.pallas_call(
        kernel,
        out_shape=tuple(jax.ShapeDtypeStruct(shape, kind) for shape, kind in out),
        in_specs=[SMEM] * smem + [VMEM] * (len(args) - smem),
        out_specs=tuple(VMEM for _ in out),
        scratch_shapes=[pltpu.VMEM(shape, kind) for shape, kind in scratch],
        compiler_params=pltpu.CompilerParams(vmem_limit_bytes=mib * 1024 * 1024),
        cost_estimate=pl.CostEstimate(flops=flops, bytes_accessed=moved, transcendentals=0),
        name=name,
    )(*args)


def inverse_rms(rows):
    return lax.rsqrt(jnp.sum(rows * rows, axis=1, keepdims=True) * (1.0 / FEATURES) + norm_eps)


def load_attend(table_ref, refs, whole):
    for part in range(2):
        for index in range(4):
            for slot in range(8):
                owner = table_ref[part, index * 8 + slot]
                whole[owner, :, part * 512 : part * 512 + 512] = refs[4 * part + index][slot]


def project_kernel(table_ref, x_ref, cos_ref, sin_ref, *refs):
    q_ref, kv0_ref, kv1_ref, gains_ref, whole, mixed = refs[8:]
    load_attend(table_ref, refs[:8], whole)
    lane = lax.broadcasted_iota(jnp.int32, (16, 128), 1)
    for tile in range(8):
        total = jnp.zeros((16, 128), jnp.float32)
        for quarter in range(4):
            piece = whole[tile * 4 + quarter, 48:64, 0:128].astype(jnp.float32)
            piece = jnp.where(lane < 32, piece, 0.0)
            total = total + (pltpu.roll(piece, 32 * quarter, 1) if quarter else piece)
        gains_ref[:, tile * 128 : tile * 128 + 128] = total[0:8]
    rows = x_ref[...].astype(jnp.float32)
    low = (rows * inverse_rms(rows) * gains_ref[2:3, :]).astype(jnp.bfloat16)
    for owner in range(CTX):
        mixed[owner * 50 : owner * 50 + 64, :] = matmul(whole[owner], low, NT)
    cosine, sine = cos_ref[...], sin_ref[...]

    def turned(start):
        front, back = mixed[start : start + 32, :], mixed[start + 32 : start + 64, :]
        return [front * cosine - back * sine, back * cosine + front * sine]

    for pair in range(8):
        pieces = turned(pair * 128)
        if pair < 7:
            pieces += turned(pair * 128 + 64)
        else:
            pieces += [jnp.zeros((64, ROWS), jnp.float32)]
        both = jnp.concatenate(pieces, axis=0) * HEAD_DIMENSION**-0.5
        q_ref[:, pair * 128 : pair * 128 + 128] = both.T.astype(jnp.bfloat16)
    for head in range(KEY_VALUE_HEADS):
        pieces = turned(960 + head * 64) + [mixed[1280 + head * 64 : 1344 + head * 64, :]]
        ref, at = (kv0_ref, head) if head < SPLIT else (kv1_ref, head - SPLIT)
        ref[:, at * 128 : at * 128 + 128] = jnp.concatenate(pieces, axis=0).T.astype(jnp.bfloat16)


def project(table, x, cosine, sine, pieces):
    return call(
        project_kernel,
        "project",
        [
            ((ROWS, WIDE), jnp.bfloat16),
            ((ROWS, SPLIT * 128), jnp.bfloat16),
            ((ROWS, KV_WIDE - SPLIT * 128), jnp.bfloat16),
            ((8, WIDE), jnp.float32),
        ],
        [((CTX, 64, WIDE), jnp.bfloat16), ((QKV + 64, ROWS), jnp.float32)],
        (table, x, cosine, sine, *pieces),
        smem=1,
        flops=2 * 2048 * 1024 * 128,
        moved=5_000_000,
    )


def load_blocks(meta_ref, refs, whole):
    for index, ref in enumerate(refs):
        lanes = slice(0, SPLIT * 128) if index < 4 else slice(SPLIT * 128, KV_WIDE)
        for slot in range(8):
            for half in range(2):
                block = meta_ref[4 + (index * 8 + slot) * 2 + half]
                rows = pl.ds(pl.multiple_of(block * BLOCK, BLOCK), BLOCK)
                whole[rows, lanes] = ref[slot, half * 64 : half * 64 + 64, :]


def head_rows(rows_ref, slot, head):
    pair = head // 2 * 128
    wide = rows_ref[pl.ds(pl.multiple_of(slot * BLOCK, BLOCK), BLOCK), pair : pair + 128]
    return wide[:, 64:] if head % 2 else wide[:, :64]


def allowed_mask(chunk, lo_block, hi_block, both):
    keys = chunk * CHUNK + lax.broadcasted_iota(jnp.int32, (CHUNK, 1), 0)
    width = WIDTH if both else HALF_WIDTH
    lane = lax.broadcasted_iota(jnp.int32, (1, width), 1)
    block = jnp.where(lane < HALF_WIDTH, lo_block, hi_block) if both else hi_block
    return keys <= block * BLOCK + lane % BLOCK


def run_chunks(meta_ref, step):
    lo_last, hi_last = meta_ref[2] // CHUNK_BLOCKS, meta_ref[3] // CHUNK_BLOCKS

    def plain(both):
        def body(chunk, carry):
            step(chunk, both, False)
            return carry

        return body

    lax.fori_loop(0, lo_last, plain(True), 0)
    step(lo_last, True, True)
    lax.fori_loop(lo_last + 1, hi_last, plain(False), 0)
    step(hi_last, False, True)
    return hi_last


def chunk_rows(chunk):
    return pl.ds(pl.multiple_of(chunk * CHUNK, CHUNK), CHUNK)


def forward_kernel(meta_ref, q_ref, *refs):
    o_ref, ot_ref, lse_ref, whole, qz, acc, peak = refs[8:]
    lo_slot, hi_slot = meta_ref[0], meta_ref[1]
    lo_block, hi_block = meta_ref[2], meta_ref[3]
    load_blocks(meta_ref, refs[:8], whole)
    for head in range(QUERY_HEADS):
        group, member = divmod(head, GROUP)
        for half, slot in enumerate((lo_slot, hi_slot)):
            rows = head_rows(q_ref, slot, head)
            start = half * HALF_WIDTH + member * BLOCK
            qz[group, start : start + BLOCK, :] = jnp.concatenate([rows, jnp.zeros_like(rows)], axis=1)
    acc[...] = jnp.zeros_like(acc)
    peak[...] = jnp.full_like(peak, NEGATIVE)
    ones_side = lax.broadcasted_iota(jnp.int32, (CHUNK, 128), 1) < HEAD_DIMENSION

    def step(chunk, both, masked):
        columns = slice(0, WIDTH) if both else slice(HALF_WIDTH, WIDTH)
        if masked:
            allowed = allowed_mask(chunk, lo_block, hi_block, both)
        for group in range(KEY_VALUE_HEADS):
            kv = whole[chunk_rows(chunk), group * 128 : group * 128 + 128]
            scores = matmul(kv, qz[group, columns, :], NT)
            if masked:
                scores = jnp.where(allowed, scores, NEGATIVE)
            old = peak[group, 0:1, columns]
            new = jnp.maximum(old, jnp.max(scores, axis=0, keepdims=True))
            exps = jnp.exp(scores - new).astype(jnp.bfloat16)
            factor = jnp.exp(old - new)
            peak[group, 0:1, columns] = new
            with_ones = jnp.where(ones_side, jnp.ones_like(kv), kv)
            acc[group, :, columns] = acc[group, :, columns] * factor + matmul(with_ones, exps, TN)

    run_chunks(meta_ref, step)
    for group in range(KEY_VALUE_HEADS):
        full = acc[group]
        total = full[0:HEAD_DIMENSION]
        out = full[HEAD_DIMENSION:] / total
        ot_ref[group] = out
        lse_ref[group] = peak[group, 0:1, :] + jnp.log(total[0:1])
        acc[group, HEAD_DIMENSION:, :] = out
    for half, slot in enumerate((lo_slot, hi_slot)):
        pieces = []
        for group in range(KEY_VALUE_HEADS):
            turned = acc[group].T[half * HALF_WIDTH : (half + 1) * HALF_WIDTH, HEAD_DIMENSION:]
            pieces += [turned[m * BLOCK : (m + 1) * BLOCK] for m in range(GROUP)]
        o_ref[pl.ds(pl.multiple_of(slot * BLOCK, BLOCK), BLOCK), :] = jnp.concatenate(pieces, axis=1)


def attention_forward(meta, q, pieces):
    return call(
        forward_kernel,
        "attend_forward",
        [
            ((ROWS, FEATURES), jnp.float32),
            ((KEY_VALUE_HEADS, HEAD_DIMENSION, WIDTH), jnp.float32),
            ((KEY_VALUE_HEADS, 1, WIDTH), jnp.float32),
        ],
        [
            ((CTX * ROWS, KV_WIDE), jnp.bfloat16),
            ((KEY_VALUE_HEADS, WIDTH, 128), jnp.bfloat16),
            ((KEY_VALUE_HEADS, 128, WIDTH), jnp.float32),
            ((KEY_VALUE_HEADS, 1, WIDTH), jnp.float32),
        ],
        (meta, q, *pieces),
        smem=1,
        flops=4 * 17 * 5 * 192 * 256 * 256,
        moved=7_000_000,
    )


def backward_kernel(
    meta_ref, q_ref, do_ref, ot_ref, lse_ref, *refs
):
    dq_ref = refs[8]
    whole, grads, qz, doz, acc, delta = refs[17:]
    lo_slot, hi_slot = meta_ref[0], meta_ref[1]
    lo_block, hi_block = meta_ref[2], meta_ref[3]
    load_blocks(meta_ref, refs[:8], whole)
    for head in range(QUERY_HEADS):
        group, member = divmod(head, GROUP)
        for half, slot in enumerate((lo_slot, hi_slot)):
            start = half * HALF_WIDTH + member * BLOCK
            rows = head_rows(q_ref, slot, head)
            qz[group, start : start + BLOCK, :] = jnp.concatenate([rows, jnp.zeros_like(rows)], axis=1)
            rows = head_rows(do_ref, slot, head)
            doz[group, start : start + BLOCK, :] = jnp.concatenate([jnp.zeros_like(rows), rows], axis=1)
    for group in range(KEY_VALUE_HEADS):
        turned = doz[group].astype(jnp.float32).T[HEAD_DIMENSION:]
        delta[group, 0:1, :] = jnp.sum(turned * ot_ref[group], axis=0, keepdims=True)
    acc[...] = jnp.zeros_like(acc)

    def step(chunk, both, masked):
        columns = slice(0, WIDTH) if both else slice(HALF_WIDTH, WIDTH)
        if masked:
            allowed = allowed_mask(chunk, lo_block, hi_block, both)
        for group in range(KEY_VALUE_HEADS):
            lanes = slice(group * 128, group * 128 + 128)
            kv = whole[chunk_rows(chunk), lanes]
            queries, upstream = qz[group, columns, :], doz[group, columns, :]
            chances = jnp.exp(matmul(kv, queries, NT) - lse_ref[group, 0:1, columns])
            if masked:
                chances = jnp.where(allowed, chances, 0.0)
            score_grad = (chances * (matmul(kv, upstream, NT) - delta[group, 0:1, columns])).astype(jnp.bfloat16)
            acc[group, :, columns] += matmul(kv, score_grad, TN)
            out = matmul(score_grad, queries, NN) + matmul(chances.astype(jnp.bfloat16), upstream, NN)
            grads[chunk_rows(chunk), lanes] = out.astype(jnp.bfloat16)

    hi_last = run_chunks(meta_ref, step)

    def clear(chunk, carry):
        grads[chunk_rows(chunk), :] = jnp.zeros((CHUNK, KV_WIDE), jnp.bfloat16)
        return carry

    lax.fori_loop(hi_last + 1, CTX * ROWS // CHUNK, clear, 0)
    for index, ref in enumerate(refs[9:17]):
        lanes = slice(0, SPLIT * 128) if index < 4 else slice(SPLIT * 128, KV_WIDE)
        for slot in range(8):
            for half in range(2):
                block = meta_ref[4 + (index * 8 + slot) * 2 + half]
                rows = pl.ds(pl.multiple_of(block * BLOCK, BLOCK), BLOCK)
                ref[slot, half * 64 : half * 64 + 64, :] = grads[rows, lanes]
    low_first = lo_slot == 0
    for head in range(QUERY_HEADS):
        group, member = divmod(head, GROUP)
        low = acc[group, 0:HEAD_DIMENSION, member * BLOCK : member * BLOCK + BLOCK]
        high = acc[group, 0:HEAD_DIMENSION, HALF_WIDTH + member * BLOCK : HALF_WIDTH + member * BLOCK + BLOCK]
        ordered = jnp.where(
            low_first, jnp.concatenate([low, high], axis=1), jnp.concatenate([high, low], axis=1)
        )
        dq_ref[head * 64 : head * 64 + 64, :] = ordered * HEAD_DIMENSION**-0.5


def attention_backward(meta, q, do, ot, lse, pieces):
    first = ((8, ROWS, SPLIT * 128), jnp.bfloat16)
    second = ((8, ROWS, KV_WIDE - SPLIT * 128), jnp.bfloat16)
    return call(
        backward_kernel,
        "attend_backward",
        [((FEATURES, ROWS), jnp.float32)] + [first] * 4 + [second] * 4,
        [
            ((CTX * ROWS, KV_WIDE), jnp.bfloat16),
            ((CTX * ROWS, KV_WIDE), jnp.bfloat16),
            ((KEY_VALUE_HEADS, WIDTH, 128), jnp.bfloat16),
            ((KEY_VALUE_HEADS, WIDTH, 128), jnp.bfloat16),
            ((KEY_VALUE_HEADS, 128, WIDTH), jnp.float32),
            ((KEY_VALUE_HEADS, 1, WIDTH), jnp.float32),
        ],
        (meta, q, do, ot, lse, *pieces),
        smem=1,
        flops=10 * 17 * 5 * 192 * 256 * 256,
        moved=13_000_000,
    )


def spread(rows):
    zeros = jnp.zeros((rows.shape[0], 16), rows.dtype)
    pieces = []
    for part in range(4):
        pieces += [rows[:, part * 240 : part * 240 + 240], zeros]
    return jnp.concatenate(pieces, axis=1)


def load_output(order_ref, refs, whole):
    core = order_ref[8]
    for side, ref in enumerate(refs):
        for part in range(4):
            lanes = pl.ds(pl.multiple_of(order_ref[side * 4 + part] * 256, 256), 256)
            for slot in range(CHIPS):
                row = pl.multiple_of(order_ref[25 + 16 * side + slot] * 64 + (core ^ side) * 32, 32)
                whole[pl.ds(row, 32), lanes] = ref[slot, :, part * 256 : part * 256 + 256]


def middle_kernel(order_ref, x_ref, o_ref, gains_ref, w0, w1, mid_ref, low_ref, ob_ref, whole):
    load_output(order_ref, (w0, w1), whole)
    wide = spread(o_ref[...]).astype(jnp.bfloat16)
    ob_ref[...] = wide
    middle = x_ref[...].astype(jnp.float32) + matmul(wide, whole[...], NT)
    mid_ref[...] = middle
    low_ref[...] = (middle * inverse_rms(middle) * gains_ref[3:4, :]).astype(jnp.bfloat16)


def middle_forward(order, x, attended, gains, own, other):
    return call(
        middle_kernel,
        "middle_forward",
        [((ROWS, WIDE), jnp.float32), ((ROWS, WIDE), jnp.bfloat16), ((ROWS, WIDE), jnp.bfloat16)],
        [((WIDE, WIDE), jnp.bfloat16)],
        (order, x, attended, gains, own, other),
        smem=1,
        flops=2 * 128 * 1024 * 1024,
        moved=4_000_000,
    )


def feed_kernel(
    order_ref, h0, h1, d0, d1, w0, w1, w2, w3, y0, y1, b0, b1, e0, e1, e23,
    both_w, down_w, both_g, down_g, ysum, bsum,
):
    weights, grads = (w0, w1, w2, w3), (e0, e1, e23.at[0], e23.at[1])
    for part, ref in enumerate(weights):
        lanes = pl.ds(pl.multiple_of(order_ref[part] * 256, 256), 256)
        for slot in range(CHIPS):
            row = pl.multiple_of(order_ref[9 + slot] * UNIT, UNIT)
            both_w[pl.ds(row, REST_CUT), lanes] = ref[slot, 0:REST_CUT, :]
            row = pl.multiple_of(order_ref[25 + slot] * UNIT + REST_CUT, 16)
            both_w[pl.ds(row, UNIT - REST_CUT), lanes] = ref[slot, REST_CUT:UNIT, :]
        for pair in range(8):
            for half in range(2):
                left = ref[order_ref[57 + 2 * pair], 192:272, half * 128 : half * 128 + 128]
                right = ref[order_ref[58 + 2 * pair], 192:272, half * 128 : half * 128 + 128]
                for side in range(2):
                    row = pl.multiple_of(order_ref[part] * (2 * UNIT) + UNIT * side + 80 * half, 16)
                    pick = slice(side * 64, side * 64 + 64)
                    down_w[pl.ds(row, 80), pair * 128 : pair * 128 + 128] = jnp.concatenate(
                        [left[:, pick], right[:, pick]], axis=1
                    )
    hidden_in = jnp.concatenate([h0[...], h1[...]], axis=0)
    upstream = jnp.concatenate([d0[...], d1[...]], axis=0)
    ysum[...] = jnp.zeros_like(ysum)
    bsum[...] = jnp.zeros_like(bsum)

    def tile(index, carry):
        rows = pl.ds(pl.multiple_of(index * TILE_FF, TILE_FF), TILE_FF)
        up_at = pl.ds(pl.multiple_of(OWN_FF + index * TILE_FF, TILE_FF), TILE_FF)
        gate_rows, up_rows, down_rows = both_w[rows, :], both_w[up_at, :], down_w[rows, :]
        gate = matmul(hidden_in, gate_rows, NT)
        up = matmul(hidden_in, up_rows, NT)
        sigmoid = jax.nn.sigmoid(gate)
        active = gate * sigmoid
        hidden = (active * up).astype(jnp.bfloat16)
        back = matmul(upstream, down_rows, NT)
        gate_back = (back * up * sigmoid * (1.0 + gate * (1.0 - sigmoid))).astype(jnp.bfloat16)
        up_back = (back * active).astype(jnp.bfloat16)
        ysum[...] += matmul(hidden, down_rows, NN)
        bsum[...] += matmul(gate_back, gate_rows, NN) + matmul(up_back, up_rows, NN)
        down_g[rows, :] = matmul(hidden, upstream, TN).astype(jnp.bfloat16)
        both_g[rows, :] = matmul(gate_back, hidden_in, TN).astype(jnp.bfloat16)
        both_g[up_at, :] = matmul(up_back, hidden_in, TN).astype(jnp.bfloat16)
        return carry

    lax.fori_loop(0, OWN_FF // TILE_FF, tile, 0)
    y0[...] = ysum[0:ROWS, :]
    y1[...] = ysum[ROWS:, :].astype(jnp.bfloat16)
    b0[...] = bsum[0:ROWS, :]
    b1[...] = bsum[ROWS:, :].astype(jnp.bfloat16)
    for part, ref in enumerate(grads):
        lanes = pl.ds(pl.multiple_of(order_ref[part] * 256, 256), 256)
        for slot in range(CHIPS):
            row = pl.multiple_of(order_ref[9 + slot] * UNIT, UNIT)
            ref[slot, 0:GRAD_CUT, :] = both_g[pl.ds(row, GRAD_CUT), lanes]
            row = pl.multiple_of(order_ref[25 + slot] * UNIT + GRAD_CUT, 32)
            ref[slot, GRAD_CUT:UNIT, :] = both_g[pl.ds(row, UNIT - GRAD_CUT), lanes]
        for pair in range(8):
            for half in range(2):
                row = pl.multiple_of(order_ref[part] * (2 * UNIT) + 80 * half, 16)
                even = down_g[pl.ds(row, 80), pair * 128 : pair * 128 + 128]
                odd = down_g[pl.ds(row + UNIT, 80), pair * 128 : pair * 128 + 128]
                to = slice(half * 128, half * 128 + 128)
                ref[order_ref[57 + 2 * pair], 160:240, to] = jnp.concatenate([even[:, :64], odd[:, :64]], axis=1)
                ref[order_ref[58 + 2 * pair], 160:240, to] = jnp.concatenate([even[:, 64:], odd[:, 64:]], axis=1)


def feed(order, own_low, other_low, own_up, other_up, weights):
    matrix = ((OWN_FF, WIDE), jnp.bfloat16)
    return call(
        feed_kernel,
        "feed",
        [
            ((ROWS, WIDE), jnp.float32),
            ((ROWS, WIDE), jnp.bfloat16),
            ((ROWS, WIDE), jnp.float32),
            ((ROWS, WIDE), jnp.bfloat16),
        ]
        + [((CHIPS, GRAD_ROWS, 256), jnp.bfloat16)] * 2
        + [((2, CHIPS, GRAD_ROWS, 256), jnp.bfloat16)],
        [((FF, WIDE), jnp.bfloat16), matrix] * 2 + [((2 * ROWS, WIDE), jnp.float32)] * 2,
        (order, own_low, other_low, own_up, other_up, *weights),
        smem=1,
        flops=2 * 9 * 256 * 1024 * 1280,
        moved=22_000_000,
        mib=52,
    )


def norm_back(grad, rows, gain):
    scale = inverse_rms(rows)
    unit = rows * scale
    unit_grad = grad * gain
    mean = jnp.sum(unit_grad * unit, axis=1, keepdims=True) * (1.0 / FEATURES)
    return scale * (unit_grad - unit * mean), jnp.sum(grad * unit, axis=0, keepdims=True)


def middle_back_kernel(
    order_ref, b_ref, more_ref, mid_ref, up_ref, gains_ref, ob_ref, w0, w1, dx_ref, do_ref, dg_ref, grad_ref, whole
):
    load_output(order_ref, (w0, w1), whole)
    back, gain_grad = norm_back(b_ref[...] + more_ref[...].astype(jnp.float32), mid_ref[...], gains_ref[3:4, :])
    dg_ref[...] = gain_grad
    dx = up_ref[...].astype(jnp.float32) + back
    dx_ref[...] = dx
    low = dx.astype(jnp.bfloat16)
    wide = matmul(low, whole[...], NN)
    pieces = [wide[:, part * 256 : part * 256 + 240] for part in range(4)]
    pieces += [jnp.zeros((ROWS, 64), jnp.float32)]
    do_ref[...] = jnp.concatenate(pieces, axis=1).astype(jnp.bfloat16)
    grad_ref[...] = matmul(low, ob_ref[...], TN).astype(jnp.bfloat16)


def middle_backward(order, back, more, middle, upstream, gains, ob, own, other):
    return call(
        middle_back_kernel,
        "middle_backward",
        [
            ((ROWS, WIDE), jnp.float32),
            ((ROWS, WIDE), jnp.bfloat16),
            ((1, WIDE), jnp.float32),
            ((WIDE, WIDE), jnp.bfloat16),
        ],
        [((WIDE, WIDE), jnp.bfloat16)],
        (order, back, more, middle, upstream, gains, ob, own, other),
        smem=1,
        flops=4 * 128 * 1024 * 1024,
        moved=8_000_000,
    )


def project_back_kernel(
    table_ref, x_ref, gains_ref, dx_ref, dg2_ref, dq_ref, dkv0_ref, dkv1_ref, go_ref, cos_ref, sin_ref, *refs
):
    grad_ref = refs[8]
    whole, mixed, low_mixed, gain_tiles = refs[17:]
    load_attend(table_ref, refs[:8], whole)
    cosine, sine = cos_ref[...], sin_ref[...]

    def turn_back(front, back, start):
        mixed[start : start + 32, :] = front * cosine + back * sine
        mixed[start + 32 : start + 64, :] = back * cosine - front * sine

    for head in range(QUERY_HEADS):
        turn_back(dq_ref[head * 64 : head * 64 + 32, :], dq_ref[head * 64 + 32 : head * 64 + 64, :], head * 64)
    for head in range(KEY_VALUE_HEADS):
        ref, at = (dkv0_ref, head) if head < SPLIT else (dkv1_ref, head - SPLIT)
        both = ref[:, at * 128 : at * 128 + 128].astype(jnp.float32).T
        turn_back(both[0:32], both[32:64], 960 + head * 64)
        mixed[1280 + head * 64 : 1344 + head * 64, :] = both[64:]
    mixed[QKV:, :] = jnp.zeros((64, ROWS), jnp.float32)
    keep = lax.broadcasted_iota(jnp.int32, (64, ROWS), 0) < 50
    for owner in range(CTX):
        low_mixed[owner] = jnp.where(keep, mixed[owner * 50 : owner * 50 + 64, :], 0.0).astype(jnp.bfloat16)
    rows = x_ref[...].astype(jnp.float32)
    low = (rows * inverse_rms(rows) * gains_ref[2:3, :]).astype(jnp.bfloat16)
    total = jnp.zeros((ROWS, WIDE), jnp.float32)
    for quarter in range(4):
        left = low_mixed[quarter * 8 : quarter * 8 + 8].reshape(512, ROWS)
        right = whole[quarter * 8 : quarter * 8 + 8].reshape(512, WIDE)
        total = total + matmul(left, right, TN)
    back, gain_grad = norm_back(total, rows, gains_ref[2:3, :])
    grad_ref[...] = dx_ref[...] + back
    row = lax.broadcasted_iota(jnp.int32, (16, 128), 0)
    lane = lax.broadcasted_iota(jnp.int32, (16, 128), 1)
    for owner in range(CTX):
        lanes = slice(owner // 4 * 128, owner // 4 * 128 + 128)
        tile = jnp.where(row == 2, gain_grad[:, lanes], 0.0) + jnp.where(row == 3, dg2_ref[:, lanes], 0.0)
        if owner % 4:
            tile = pltpu.roll(tile, 128 - 32 * (owner % 4), 1)
        gain_tiles[owner] = jnp.where(lane < 32, tile, 0.0)
    for quarter in range(4):
        left = low_mixed[quarter * 8 : quarter * 8 + 8].reshape(512, ROWS)
        whole[quarter * 8 : quarter * 8 + 8] = matmul(left, low, NN).astype(jnp.bfloat16).reshape(8, 64, WIDE)
    for owner in range(CTX):
        whole[owner, 48:64, 0:128] = (whole[owner, 48:64, 0:128].astype(jnp.float32) + gain_tiles[owner]).astype(
            jnp.bfloat16
        )
    for part in range(2):
        for index in range(4):
            for slot in range(8):
                owner = table_ref[part, index * 8 + slot]
                lanes = slice(part * 512, part * 512 + 512)
                ref = refs[9 + 4 * part + index]
                ref[slot, 0:64, :] = whole[owner, :, lanes]
                ref[slot, 64:96, :] = go_ref[pl.ds(pl.multiple_of(owner * 32, 32), 32), lanes]


def project_backward(table, x, gains, dx, dg2, dq, dkv, output_grad, cosine, sine, pieces):
    piece = ((8, 96, 512), jnp.bfloat16)
    return call(
        project_back_kernel,
        "project_backward",
        [((ROWS, WIDE), jnp.float32)] + [piece] * 8,
        [
            ((CTX, 64, WIDE), jnp.bfloat16),
            ((QKV + 64, ROWS), jnp.float32),
            ((CTX, 64, ROWS), jnp.bfloat16),
            ((CTX, 16, 128), jnp.float32),
        ],
        (table, x, gains, dx, dg2, dq, *dkv, output_grad, cosine, sine, *pieces),
        smem=1,
        flops=4 * 2048 * 1024 * 128,
        moved=10_000_000,
    )


def rotary_tables(positions, head_size):
    half_size = head_size // 2
    inverse = jnp.power(10000.0, -2.0 * jnp.arange(half_size, dtype=jnp.float32) / head_size)
    angles = inverse[:, None] * positions.astype(jnp.float32)[None, :]
    return (jnp.cos(angles), jnp.sin(angles))


def adamw(weight, first_old, second_old, gradient, rate, decay):
    first_next = beta_one * first_old + (1.0 - beta_one) * gradient
    second_next = beta_two * second_old + (1.0 - beta_two) * gradient * gradient
    first_hat = first_next / (1.0 - beta_one**STEP)
    second_hat = second_next / (1.0 - beta_two**STEP)
    weight_next = weight - rate * (first_hat / (jnp.sqrt(second_hat) + adam_eps) + decay * weight)
    return (weight_next, first_next, second_next)


def pad_features(rows):
    count = rows.shape[-1] // 30
    shaped = rows.reshape(rows.shape[0], count, 30)
    return jnp.pad(shaped, ((0, 0), (0, 0), (0, 2))).reshape(rows.shape[0], count * 32)


def drop_features(rows):
    count = rows.shape[-1] // 32
    return rows.reshape(rows.shape[0], count, 32)[:, :, :30].reshape(rows.shape[0], count * 30)


def pad_rows(value, count):
    return jnp.pad(value, ((0, count - value.shape[0]), (0, 0)))


def total_of(pieces):
    total = pieces[0].astype(jnp.float32)
    for piece in pieces[1:]:
        total = total + piece.astype(jnp.float32)
    return total


def on_device(
    tokens,
    cotangent,
    blocks,
    attend_weight,
    output_weight,
    gateup_weight,
    down_weight,
    norm_gains,
    attend_first,
    output_first,
    gateup_first,
    down_first,
    gains_first,
    attend_second,
    output_second,
    gateup_second,
    down_second,
    gains_second,
):
    low = jnp.bfloat16
    ctx_index = lax.axis_index("ctx")
    wsh_index = lax.axis_index("wsh")
    core = ctx_index % 2

    attend_shard = pad_features(attend_weight.astype(low).T)
    gain_shard = jnp.pad(norm_gains.astype(low), ((0, 0), (0, 226)))
    attend_shard = pad_rows(jnp.concatenate([attend_shard, gain_shard], axis=0), 64)
    attend_rows = gather_rows(attend_shard, wsh_index)
    down_halves = jnp.pad(down_weight.astype(low), ((0, 0), (0, 2))).reshape(2, 2, UNIT, 32)
    mine = lax.dynamic_index_in_dim(down_halves, core, axis=1, keepdims=False)
    theirs = swap(lax.dynamic_index_in_dim(down_halves, 1 - core, axis=1, keepdims=False), SIBLING)
    upper = core == 1
    joined = jnp.stack([jnp.where(upper, theirs, mine), jnp.where(upper, mine, theirs)], axis=2)
    down_shard = joined.reshape(2, 2, 80, 64).transpose(2, 1, 0, 3).reshape(80, 256)
    gateup_shard = pad_features(gateup_weight.astype(low).T)
    output_shard = jnp.pad(output_weight.astype(low).T, ((0, 2), (0, 16)))
    rest_shard = jnp.concatenate([gateup_shard, output_shard, down_shard], axis=0)
    parts, rest_parts = gather_both(
        [attend_rows[:, :512], attend_rows[:, 512:]], [rest_shard[:REST_CUT], rest_shard[REST_CUT:]]
    )
    attend_pieces = [piece for pair in parts for piece in pair]
    orders = [
        lax.dynamic_index_in_dim(
            jnp.asarray(ROW_ORDER.reshape(8, 4)), (core ^ side) * 4 + wsh_index, axis=0, keepdims=False
        )
        for side in range(2)
    ]
    chips = lax.dynamic_index_in_dim(jnp.asarray(CHIP_ORDER), ctx_index, axis=0, keepdims=False)
    order = jnp.concatenate([*orders, core.reshape(1), chips]).astype(jnp.int32)

    upstream = pad_features(cotangent[0])
    upstream_other = swap(upstream, SIBLING)
    x = after(pad_features(tokens[0]), upstream_other)

    position_index = jnp.arange(2 * CTX, dtype=jnp.int32)
    mine_pair = lax.dynamic_slice_in_dim(blocks, 2 * ctx_index, 2)
    offsets = jnp.arange(BLOCK, dtype=jnp.int32)
    positions = (mine_pair[:, None] * BLOCK + offsets[None, :]).reshape(ROWS)
    cosine, sine = rotary_tables(positions, HEAD_DIMENSION)
    owners = jnp.stack(
        [lax.dynamic_index_in_dim(jnp.asarray(table), ctx_index, axis=0, keepdims=False) for table in ORIGINS]
    )
    slots = owners[:, :, None] * 2 + jnp.arange(2, dtype=jnp.int32)
    held = jnp.sum(
        jnp.where(slots.reshape(2, 64)[:, :, None] == position_index, blocks[None, None, :], 0), axis=2
    )
    lo_slot = (mine_pair[0] > mine_pair[1]).astype(jnp.int32)
    own_blocks = jnp.stack([lo_slot, 1 - lo_slot, jnp.min(mine_pair), jnp.max(mine_pair)])
    meta = jnp.concatenate([own_blocks, held[0], held[1]]).astype(jnp.int32)

    q, keys_first, keys_second, gains = project(owners, x, cosine, sine, attend_pieces)
    rest_parts = after(rest_parts, q)
    rest_own = jnp.concatenate([jnp.concatenate(pair, axis=0) for pair in rest_parts], axis=1)
    rest_first, rest_second = swap_rows(rest_own, 0), swap_rows(rest_own, 1)
    kv_first, kv_second = gather_chips([keys_first, keys_second])
    rest_third = swap_rows(after(rest_first, kv_first[0]), 1)
    attended, attended_turned, log_total = attention_forward(meta, q, [*kv_first, *kv_second])
    rest_pieces = (rest_own, rest_first, rest_second, rest_third)
    output_own = jnp.concatenate([piece[:, 160:192, :] for piece in after(rest_pieces, attended)], axis=2)
    output_other = swap(output_own, SIBLING)
    middle, second_low, attended_wide = middle_forward(
        order, x, attended, gains, output_own, output_other
    )
    second_other = swap(second_low, SIBLING)
    own_y, other_y, own_back, other_back, *rest_grads = feed(
        order, second_low, second_other, upstream, upstream_other, rest_pieces
    )
    back_more = swap(other_back, SIBLING)
    y_more = swap(other_y, SIBLING)
    rest_got = swap_rows(rest_grads[2], 1)
    middle_grad, attended_reverse, gain_second_grad, output_grad = middle_backward(
        order, own_back, back_more, middle, upstream, gains, attended_wide, output_own, output_other
    )
    result = middle + own_y + y_more.astype(jnp.float32)
    layer_output = drop_features(result.astype(low))[None]

    query_grad, *key_value_grads = attention_backward(
        meta, q, attended_reverse, attended_turned, log_total, [*kv_first, *kv_second]
    )
    rest_more = swap_rows(add(rest_grads[1], rest_got[1]), 0)
    kv_grads = scatter_chips(
        [key_value_grads[:4], key_value_grads[4:]], (rest_got, (), rest_more)
    )
    rest_state = []
    for plan, rows in zip(PLANS, (slice(0, GRAD_CUT), slice(GRAD_CUT, GRAD_ROWS))):
        arrays = [array[:, rows, :] for array in (rest_grads[0], rest_got[0], rest_more)]
        kept, sent = [
            total_of([array[half] for array in arrays]).astype(low) for half in (slice(0, 8), slice(8, 16))
        ]
        rest_state.append((kept, swap(sent, plan[3])))
    input_grad, *attend_grads = project_backward(
        owners,
        x,
        gains,
        middle_grad,
        gain_second_grad,
        query_grad,
        kv_grads,
        output_grad,
        cosine,
        sine,
        attend_pieces,
    )
    input_grad = drop_features(input_grad)[None]

    attend_low, attend_high, rest_low, rest_high = scatter_chips(
        [attend_grads[:4], attend_grads[4:]], rest=rest_state
    )
    rest_total = jnp.concatenate([rest_low, rest_high], axis=0).astype(jnp.float32)
    gateup_sum = drop_features(rest_total[0:160]).T
    down_total = rest_total[160:].reshape(80, 2, 2, 2, 32).transpose(2, 1, 0, 3, 4).reshape(2, UNIT, 2, 32)
    down_mine = lax.dynamic_index_in_dim(down_total, core, axis=2, keepdims=False)
    down_theirs = lax.dynamic_index_in_dim(down_total, 1 - core, axis=2, keepdims=False)
    down_got = swap(down_theirs.astype(low), SIBLING).astype(jnp.float32)
    down_sum = jnp.stack([jnp.where(upper, down_got, down_mine), jnp.where(upper, down_mine, down_got)], axis=1)
    down_sum = down_sum.reshape(640, 32)[:, :30]

    attend_rows_sum = jnp.concatenate([attend_low, attend_high], axis=1)
    row_index = jnp.arange(96, dtype=jnp.int32)[:, None]
    attend_parts = scatter_rows(attend_rows_sum, wsh_index, (row_index == 50) | (row_index == 51))
    attend_total = total_of(attend_parts)
    attend_sum = drop_features(attend_total[0:50]).T
    output_total = attend_total[64:94, :240].T
    stacked = jnp.stack([part[50:52, :30] for part in attend_parts]).astype(jnp.float32)
    gains_sum = total_of(
        [lax.dynamic_index_in_dim(stacked, (wsh_index - source) % 4, axis=0, keepdims=False) for source in range(4)]
    )

    output_rate = max(1, QUERY_HEADS * HEAD_DIMENSION * 32 // (CTX * ROWS)) ** (-0.5)
    attend_next = adamw(attend_weight, attend_first, attend_second, attend_sum, 0.02, 0.1)
    output_next = adamw(output_weight, output_first, output_second, output_total, output_rate, 0.1)
    gateup_next = adamw(gateup_weight, gateup_first, gateup_second, gateup_sum, 0.02, 0.1)
    down_next = adamw(down_weight, down_first, down_second, down_sum, 0.02, 0.1)
    gains_next = adamw(norm_gains, gains_first, gains_second, gains_sum, 0.7, 0.0)
    return (layer_output, input_grad, *attend_next, *output_next, *gateup_next, *down_next, *gains_next)


def solution(mesh):
    rows, columns, both = P("wsh", "ctx", None), P(None, "ctx"), P("wsh", "ctx")
    weights = (both, both, both, both, columns)
    return jax.shard_map(
        on_device,
        mesh=mesh,
        in_specs=(rows, rows, P(), *weights, *weights, *weights),
        out_specs=(rows, rows, *([both] * 12), *([columns] * 3)),
        check_vma=False,
    )
```

```python
import numpy as np
import jax
import jax.numpy as jnp
from jax import lax
from jax.experimental import pallas as pl
from jax.experimental.pallas import tpu as pltpu
from jax.sharding import PartitionSpec as P

QUERY_HEADS = 15
KEY_VALUE_HEADS = 5
HEAD_DIMENSION = 64
GROUP = 3
BLOCK = 64
CHUNK_BLOCKS = 4
CHUNK = BLOCK * CHUNK_BLOCKS
HALF_WIDTH = GROUP * BLOCK
WIDTH = 2 * HALF_WIDTH
NEGATIVE = -1e30
FF = 2560
STEP = 5
ROWS = 128
WIDE = 1024
FEATURES = 960
KV_WIDE = 640
SPLIT = 3
QKV = 1600
CTX = 32
CHIPS = 16
OWN_FF = FF // 2
TILE_FF = 256
UNIT = 160
GRAD_ROWS = 240
GRAD_CUT = 128
REST_CUT = 144
NT = (((1,), (1,)), ((), ()))
TN = (((0,), (0,)), ((), ()))
NN = (((1,), (0,)), ((), ()))

beta_one = 0.9
beta_two = 0.95
adam_eps = 1e-08
norm_eps = 1e-05


def place(index):
    return index // 8, index // 2 % 4, index % 2


def index_of(z, x, core):
    return (z * 4 + x) * 2 + core


def neighbour(value, pairing):
    if pairing == 0:
        return value ^ 1
    return (value + 1) % 4 if value % 2 else (value - 1) % 4


def partner_list(axis, step):
    partners = []
    for index in range(CTX):
        z, x, core = place(index)
        pairing = step ^ core
        if axis == "z":
            partners.append(index_of(neighbour(z, pairing), x, core))
        else:
            partners.append(index_of(z, neighbour(x, pairing), core))
    return partners


PLANS = (
    [partner_list("x", 0), partner_list("x", 1), partner_list("z", 0), partner_list("z", 1)],
    [partner_list("z", 0), partner_list("z", 1), partner_list("x", 0), partner_list("x", 1)],
)
SIBLING = [index ^ 1 for index in range(CTX)]


def origins(plan):
    held = [[index] for index in range(CTX)]
    for partners in plan:
        held = [held[index] + held[partners[index]] for index in range(CTX)]
    held = [held[index] + held[SIBLING[index]] for index in range(CTX)]
    return np.array(held, np.int32)


ORIGINS = [origins(plan) for plan in PLANS]
CHIP_ORDER = np.concatenate(
    [
        ORIGINS[0][:, :CHIPS] // 2,
        ORIGINS[1][:, :CHIPS] // 2,
        ORIGINS[1][SIBLING, :CHIPS] // 2,
        np.argsort(ORIGINS[1][:, :CHIPS] // 2, axis=1),
    ],
    axis=1,
).astype(np.int32)


def swap(value, partners):
    return lax.ppermute(value, "ctx", [(source, target) for source, target in enumerate(partners)])


def after(value, *others):
    return lax.optimization_barrier((value, *others))[0]


def swap_all(values, step):
    return [swap(value, plan[step]) for value, plan in zip(values, PLANS)]


def join(values, got):
    return [jnp.concatenate([value, more], axis=0) for value, more in zip(values, got)]


def core_swap(values, got):
    return [(value, more, swap(value, SIBLING), swap(more, SIBLING)) for value, more in zip(values, got)]


def gather_chips(parts):
    values = [part[None] for part in parts]
    for step in range(3):
        values = join(values, lax.optimization_barrier(swap_all(values, step)))
    return core_swap(values, swap_all(values, 3))


def gather_both(parts, rest):
    values, others = [part[None] for part in parts], [part[None] for part in rest]
    values = join(values, lax.optimization_barrier(swap_all(values, 0)))
    for step in (1, 2):
        got, more = lax.optimization_barrier((swap_all(values, step), swap_all(others, step - 1)))
        values, others = join(values, got), join(others, more)
    got, more = swap_all(values, 3), swap_all(others, 2)
    return core_swap(values, got), (others, more)


def add(left, right):
    return (left.astype(jnp.float32) + right.astype(jnp.float32)).astype(jnp.bfloat16)


def scatter_core(parts):
    state = []
    for (low, high, other_low, other_high), plan in zip(parts, PLANS):
        got_high, got_low = swap(other_high, SIBLING), swap(other_low, SIBLING)
        state.append((add(low, got_low), swap(add(high, got_high), plan[3])))
    return state


def scatter_step(state, step):
    following = []
    for (kept, got), plan in zip(state, PLANS):
        half = kept.shape[0] // 2
        more = swap(add(kept[half:], got[half:]), plan[step])
        following.append((add(kept[:half], got[:half]), more))
    return following


def scatter_chips(parts, beside=((), (), ()), rest=()):
    state = scatter_core(parts)
    for step in reversed(range(3)):
        state, rest = lax.optimization_barrier((state, rest, beside[2 - step]))[:2]
        state, rest = scatter_step(state, step), scatter_step(rest, step) if rest else rest
    return [add(kept, got)[0] for kept, got in [*state, *rest]]


def row_partners(step):
    return [neighbour(index % 4, step ^ (index // 4 % 2)) for index in range(4 * CTX)]


def swap_rows(value, step):
    pairs = [(index, index // 4 * 4 + target) for index, target in enumerate(row_partners(step))]
    return lax.ppermute(value, ("ctx", "wsh"), pairs)


def row_order(core, wsh):
    first, second = neighbour(wsh, core), neighbour(wsh, 1 - core)
    return [wsh, first, second, neighbour(second, core)]


ROW_ORDER = np.array([[row_order(core, wsh) for wsh in range(4)] for core in range(2)], np.int32)


def gather_rows(value, wsh_index):
    for bit in (1, 2):
        more = lax.ppermute(value, "wsh", [(source, source ^ bit) for source in range(4)])
        upper = (wsh_index & bit) != 0
        value = jnp.concatenate([jnp.where(upper, more, value), jnp.where(upper, value, more)], axis=1)
    return value


def scatter_rows(value, wsh_index, shared=None):
    pieces = []
    for step in range(4):
        start = (wsh_index + step) % 4 * 256
        piece = lax.dynamic_slice_in_dim(value, start, 256, axis=1)
        if shared is not None:
            piece = jnp.where(shared, value[:, :256], piece)
        if step:
            piece = lax.ppermute(piece, "wsh", [(source, (source + step) % 4) for source in range(4)])
        pieces.append(piece)
    return pieces


def matmul(left, right, dims):
    return lax.dot_general(left, right, dims, preferred_element_type=jnp.float32)


VMEM = pl.BlockSpec(memory_space=pltpu.VMEM)
SMEM = pl.BlockSpec(memory_space=pltpu.SMEM)


def call(kernel, name, out, scratch, args, smem=0, flops=0, moved=0, mib=40):
    return pl.pallas_call(
        kernel,
        out_shape=tuple(jax.ShapeDtypeStruct(shape, kind) for shape, kind in out),
        in_specs=[SMEM] * smem + [VMEM] * (len(args) - smem),
        out_specs=tuple(VMEM for _ in out),
        scratch_shapes=[pltpu.VMEM(shape, kind) for shape, kind in scratch],
        compiler_params=pltpu.CompilerParams(vmem_limit_bytes=mib * 1024 * 1024),
        cost_estimate=pl.CostEstimate(flops=flops, bytes_accessed=moved, transcendentals=0),
        name=name,
    )(*args)


def inverse_rms(rows):
    return lax.rsqrt(jnp.sum(rows * rows, axis=1, keepdims=True) * (1.0 / FEATURES) + norm_eps)


def load_attend(table_ref, refs, whole):
    for part in range(2):
        for index in range(4):
            for slot in range(8):
                owner = table_ref[part, index * 8 + slot]
                whole[owner, :, part * 512 : part * 512 + 512] = refs[4 * part + index][slot]


def project_kernel(table_ref, x_ref, cos_ref, sin_ref, *refs):
    q_ref, kv0_ref, kv1_ref, gains_ref, whole, mixed = refs[8:]
    load_attend(table_ref, refs[:8], whole)
    lane = lax.broadcasted_iota(jnp.int32, (16, 128), 1)
    for tile in range(8):
        total = jnp.zeros((16, 128), jnp.float32)
        for quarter in range(4):
            piece = whole[tile * 4 + quarter, 48:64, 0:128].astype(jnp.float32)
            piece = jnp.where(lane < 32, piece, 0.0)
            total = total + (pltpu.roll(piece, 32 * quarter, 1) if quarter else piece)
        gains_ref[:, tile * 128 : tile * 128 + 128] = total[0:8]
    rows = x_ref[...].astype(jnp.float32)
    low = (rows * inverse_rms(rows) * gains_ref[2:3, :]).astype(jnp.bfloat16)
    for owner in range(CTX):
        mixed[owner * 50 : owner * 50 + 64, :] = matmul(whole[owner], low, NT)
    cosine, sine = cos_ref[...], sin_ref[...]

    def turned(start):
        front, back = mixed[start : start + 32, :], mixed[start + 32 : start + 64, :]
        return [front * cosine - back * sine, back * cosine + front * sine]

    for pair in range(8):
        pieces = turned(pair * 128)
        if pair < 7:
            pieces += turned(pair * 128 + 64)
        else:
            pieces += [jnp.zeros((64, ROWS), jnp.float32)]
        both = jnp.concatenate(pieces, axis=0) * HEAD_DIMENSION**-0.5
        q_ref[:, pair * 128 : pair * 128 + 128] = both.T.astype(jnp.bfloat16)
    for head in range(KEY_VALUE_HEADS):
        pieces = turned(960 + head * 64) + [mixed[1280 + head * 64 : 1344 + head * 64, :]]
        ref, at = (kv0_ref, head) if head < SPLIT else (kv1_ref, head - SPLIT)
        ref[:, at * 128 : at * 128 + 128] = jnp.concatenate(pieces, axis=0).T.astype(jnp.bfloat16)


def project(table, x, cosine, sine, pieces):
    return call(
        project_kernel,
        "project",
        [
            ((ROWS, WIDE), jnp.bfloat16),
            ((ROWS, SPLIT * 128), jnp.bfloat16),
            ((ROWS, KV_WIDE - SPLIT * 128), jnp.bfloat16),
            ((8, WIDE), jnp.float32),
        ],
        [((CTX, 64, WIDE), jnp.bfloat16), ((QKV + 64, ROWS), jnp.float32)],
        (table, x, cosine, sine, *pieces),
        smem=1,
        flops=2 * 2048 * 1024 * 128,
        moved=5_000_000,
    )


def load_blocks(meta_ref, refs, whole):
    for index, ref in enumerate(refs):
        lanes = slice(0, SPLIT * 128) if index < 4 else slice(SPLIT * 128, KV_WIDE)
        for slot in range(8):
            for half in range(2):
                block = meta_ref[4 + (index * 8 + slot) * 2 + half]
                rows = pl.ds(pl.multiple_of(block * BLOCK, BLOCK), BLOCK)
                whole[rows, lanes] = ref[slot, half * 64 : half * 64 + 64, :]


def head_rows(rows_ref, slot, head):
    pair = head // 2 * 128
    wide = rows_ref[pl.ds(pl.multiple_of(slot * BLOCK, BLOCK), BLOCK), pair : pair + 128]
    return wide[:, 64:] if head % 2 else wide[:, :64]


def allowed_mask(chunk, lo_block, hi_block, both):
    keys = chunk * CHUNK + lax.broadcasted_iota(jnp.int32, (CHUNK, 1), 0)
    width = WIDTH if both else HALF_WIDTH
    lane = lax.broadcasted_iota(jnp.int32, (1, width), 1)
    block = jnp.where(lane < HALF_WIDTH, lo_block, hi_block) if both else hi_block
    return keys <= block * BLOCK + lane % BLOCK


def run_chunks(meta_ref, step):
    lo_last, hi_last = meta_ref[2] // CHUNK_BLOCKS, meta_ref[3] // CHUNK_BLOCKS

    def plain(both):
        def body(chunk, carry):
            step(chunk, both, False)
            return carry

        return body

    lax.fori_loop(0, lo_last, plain(True), 0)
    step(lo_last, True, True)
    lax.fori_loop(lo_last + 1, hi_last, plain(False), 0)
    step(hi_last, False, True)
    return hi_last


def chunk_rows(chunk):
    return pl.ds(pl.multiple_of(chunk * CHUNK, CHUNK), CHUNK)


def forward_kernel(meta_ref, q_ref, *refs):
    o_ref, ot_ref, lse_ref, whole, qz, acc, peak = refs[8:]
    lo_slot, hi_slot = meta_ref[0], meta_ref[1]
    lo_block, hi_block = meta_ref[2], meta_ref[3]
    load_blocks(meta_ref, refs[:8], whole)
    for head in range(QUERY_HEADS):
        group, member = divmod(head, GROUP)
        for half, slot in enumerate((lo_slot, hi_slot)):
            rows = head_rows(q_ref, slot, head)
            start = half * HALF_WIDTH + member * BLOCK
            qz[group, start : start + BLOCK, :] = jnp.concatenate([rows, jnp.zeros_like(rows)], axis=1)
    acc[...] = jnp.zeros_like(acc)
    peak[...] = jnp.full_like(peak, NEGATIVE)
    ones_side = lax.broadcasted_iota(jnp.int32, (CHUNK, 128), 1) < HEAD_DIMENSION

    def step(chunk, both, masked):
        columns = slice(0, WIDTH) if both else slice(HALF_WIDTH, WIDTH)
        if masked:
            allowed = allowed_mask(chunk, lo_block, hi_block, both)
        for group in range(KEY_VALUE_HEADS):
            kv = whole[chunk_rows(chunk), group * 128 : group * 128 + 128]
            scores = matmul(kv, qz[group, columns, :], NT)
            if masked:
                scores = jnp.where(allowed, scores, NEGATIVE)
            old = peak[group, 0:1, columns]
            new = jnp.maximum(old, jnp.max(scores, axis=0, keepdims=True))
            exps = jnp.exp(scores - new).astype(jnp.bfloat16)
            factor = jnp.exp(old - new)
            peak[group, 0:1, columns] = new
            with_ones = jnp.where(ones_side, jnp.ones_like(kv), kv)
            acc[group, :, columns] = acc[group, :, columns] * factor + matmul(with_ones, exps, TN)

    run_chunks(meta_ref, step)
    for group in range(KEY_VALUE_HEADS):
        full = acc[group]
        total = full[0:HEAD_DIMENSION]
        out = full[HEAD_DIMENSION:] / total
        ot_ref[group] = out
        lse_ref[group] = peak[group, 0:1, :] + jnp.log(total[0:1])
        acc[group, HEAD_DIMENSION:, :] = out
    for half, slot in enumerate((lo_slot, hi_slot)):
        pieces = []
        for group in range(KEY_VALUE_HEADS):
            turned = acc[group].T[half * HALF_WIDTH : (half + 1) * HALF_WIDTH, HEAD_DIMENSION:]
            pieces += [turned[m * BLOCK : (m + 1) * BLOCK] for m in range(GROUP)]
        o_ref[pl.ds(pl.multiple_of(slot * BLOCK, BLOCK), BLOCK), :] = jnp.concatenate(pieces, axis=1)


def attention_forward(meta, q, pieces):
    return call(
        forward_kernel,
        "attend_forward",
        [
            ((ROWS, FEATURES), jnp.float32),
            ((KEY_VALUE_HEADS, HEAD_DIMENSION, WIDTH), jnp.float32),
            ((KEY_VALUE_HEADS, 1, WIDTH), jnp.float32),
        ],
        [
            ((CTX * ROWS, KV_WIDE), jnp.bfloat16),
            ((KEY_VALUE_HEADS, WIDTH, 128), jnp.bfloat16),
            ((KEY_VALUE_HEADS, 128, WIDTH), jnp.float32),
            ((KEY_VALUE_HEADS, 1, WIDTH), jnp.float32),
        ],
        (meta, q, *pieces),
        smem=1,
        flops=4 * 17 * 5 * 192 * 256 * 256,
        moved=7_000_000,
    )


def backward_kernel(
    meta_ref, q_ref, do_ref, ot_ref, lse_ref, *refs
):
    dq_ref = refs[8]
    whole, grads, qz, doz, acc, delta = refs[17:]
    lo_slot, hi_slot = meta_ref[0], meta_ref[1]
    lo_block, hi_block = meta_ref[2], meta_ref[3]
    load_blocks(meta_ref, refs[:8], whole)
    for head in range(QUERY_HEADS):
        group, member = divmod(head, GROUP)
        for half, slot in enumerate((lo_slot, hi_slot)):
            start = half * HALF_WIDTH + member * BLOCK
            rows = head_rows(q_ref, slot, head)
            qz[group, start : start + BLOCK, :] = jnp.concatenate([rows, jnp.zeros_like(rows)], axis=1)
            rows = head_rows(do_ref, slot, head)
            doz[group, start : start + BLOCK, :] = jnp.concatenate([jnp.zeros_like(rows), rows], axis=1)
    for group in range(KEY_VALUE_HEADS):
        turned = doz[group].astype(jnp.float32).T[HEAD_DIMENSION:]
        delta[group, 0:1, :] = jnp.sum(turned * ot_ref[group], axis=0, keepdims=True)
    acc[...] = jnp.zeros_like(acc)

    def step(chunk, both, masked):
        columns = slice(0, WIDTH) if both else slice(HALF_WIDTH, WIDTH)
        if masked:
            allowed = allowed_mask(chunk, lo_block, hi_block, both)
        for group in range(KEY_VALUE_HEADS):
            lanes = slice(group * 128, group * 128 + 128)
            kv = whole[chunk_rows(chunk), lanes]
            queries, upstream = qz[group, columns, :], doz[group, columns, :]
            chances = jnp.exp(matmul(kv, queries, NT) - lse_ref[group, 0:1, columns])
            if masked:
                chances = jnp.where(allowed, chances, 0.0)
            score_grad = (chances * (matmul(kv, upstream, NT) - delta[group, 0:1, columns])).astype(jnp.bfloat16)
            acc[group, :, columns] += matmul(kv, score_grad, TN)
            out = matmul(score_grad, queries, NN) + matmul(chances.astype(jnp.bfloat16), upstream, NN)
            grads[chunk_rows(chunk), lanes] = out.astype(jnp.bfloat16)

    hi_last = run_chunks(meta_ref, step)

    def clear(chunk, carry):
        grads[chunk_rows(chunk), :] = jnp.zeros((CHUNK, KV_WIDE), jnp.bfloat16)
        return carry

    lax.fori_loop(hi_last + 1, CTX * ROWS // CHUNK, clear, 0)
    for index, ref in enumerate(refs[9:17]):
        lanes = slice(0, SPLIT * 128) if index < 4 else slice(SPLIT * 128, KV_WIDE)
        for slot in range(8):
            for half in range(2):
                block = meta_ref[4 + (index * 8 + slot) * 2 + half]
                rows = pl.ds(pl.multiple_of(block * BLOCK, BLOCK), BLOCK)
                ref[slot, half * 64 : half * 64 + 64, :] = grads[rows, lanes]
    low_first = lo_slot == 0
    for head in range(QUERY_HEADS):
        group, member = divmod(head, GROUP)
        low = acc[group, 0:HEAD_DIMENSION, member * BLOCK : member * BLOCK + BLOCK]
        high = acc[group, 0:HEAD_DIMENSION, HALF_WIDTH + member * BLOCK : HALF_WIDTH + member * BLOCK + BLOCK]
        ordered = jnp.where(
            low_first, jnp.concatenate([low, high], axis=1), jnp.concatenate([high, low], axis=1)
        )
        dq_ref[head * 64 : head * 64 + 64, :] = ordered * HEAD_DIMENSION**-0.5


def attention_backward(meta, q, do, ot, lse, pieces):
    first = ((8, ROWS, SPLIT * 128), jnp.bfloat16)
    second = ((8, ROWS, KV_WIDE - SPLIT * 128), jnp.bfloat16)
    return call(
        backward_kernel,
        "attend_backward",
        [((FEATURES, ROWS), jnp.float32)] + [first] * 4 + [second] * 4,
        [
            ((CTX * ROWS, KV_WIDE), jnp.bfloat16),
            ((CTX * ROWS, KV_WIDE), jnp.bfloat16),
            ((KEY_VALUE_HEADS, WIDTH, 128), jnp.bfloat16),
            ((KEY_VALUE_HEADS, WIDTH, 128), jnp.bfloat16),
            ((KEY_VALUE_HEADS, 128, WIDTH), jnp.float32),
            ((KEY_VALUE_HEADS, 1, WIDTH), jnp.float32),
        ],
        (meta, q, do, ot, lse, *pieces),
        smem=1,
        flops=10 * 17 * 5 * 192 * 256 * 256,
        moved=13_000_000,
    )


def spread(rows):
    zeros = jnp.zeros((rows.shape[0], 16), rows.dtype)
    pieces = []
    for part in range(4):
        pieces += [rows[:, part * 240 : part * 240 + 240], zeros]
    return jnp.concatenate(pieces, axis=1)


def load_output(order_ref, refs, whole):
    core = order_ref[8]
    for side, ref in enumerate(refs):
        for part in range(4):
            lanes = pl.ds(pl.multiple_of(order_ref[side * 4 + part] * 256, 256), 256)
            for slot in range(CHIPS):
                row = pl.multiple_of(order_ref[25 + 16 * side + slot] * 64 + (core ^ side) * 32, 32)
                whole[pl.ds(row, 32), lanes] = ref[slot, :, part * 256 : part * 256 + 256]


def middle_kernel(order_ref, x_ref, o_ref, gains_ref, w0, w1, mid_ref, low_ref, ob_ref, whole):
    load_output(order_ref, (w0, w1), whole)
    wide = spread(o_ref[...]).astype(jnp.bfloat16)
    ob_ref[...] = wide
    middle = x_ref[...].astype(jnp.float32) + matmul(wide, whole[...], NT)
    mid_ref[...] = middle
    low_ref[...] = (middle * inverse_rms(middle) * gains_ref[3:4, :]).astype(jnp.bfloat16)


def middle_forward(order, x, attended, gains, own, other):
    return call(
        middle_kernel,
        "middle_forward",
        [((ROWS, WIDE), jnp.float32), ((ROWS, WIDE), jnp.bfloat16), ((ROWS, WIDE), jnp.bfloat16)],
        [((WIDE, WIDE), jnp.bfloat16)],
        (order, x, attended, gains, own, other),
        smem=1,
        flops=2 * 128 * 1024 * 1024,
        moved=4_000_000,
    )


def feed_kernel(
    order_ref, h0, h1, d0, d1, w0, w1, w2, w3, y0, y1, b0, b1, e0, e1, e23,
    both_w, down_w, both_g, down_g, ysum, bsum,
):
    weights, grads = (w0, w1, w2, w3), (e0, e1, e23.at[0], e23.at[1])
    for part, ref in enumerate(weights):
        lanes = pl.ds(pl.multiple_of(order_ref[part] * 256, 256), 256)
        for slot in range(CHIPS):
            row = pl.multiple_of(order_ref[9 + slot] * UNIT, UNIT)
            both_w[pl.ds(row, REST_CUT), lanes] = ref[slot, 0:REST_CUT, :]
            row = pl.multiple_of(order_ref[25 + slot] * UNIT + REST_CUT, 16)
            both_w[pl.ds(row, UNIT - REST_CUT), lanes] = ref[slot, REST_CUT:UNIT, :]
        for pair in range(8):
            for half in range(2):
                left = ref[order_ref[57 + 2 * pair], 192:272, half * 128 : half * 128 + 128]
                right = ref[order_ref[58 + 2 * pair], 192:272, half * 128 : half * 128 + 128]
                for side in range(2):
                    row = pl.multiple_of(order_ref[part] * (2 * UNIT) + UNIT * side + 80 * half, 16)
                    pick = slice(side * 64, side * 64 + 64)
                    down_w[pl.ds(row, 80), pair * 128 : pair * 128 + 128] = jnp.concatenate(
                        [left[:, pick], right[:, pick]], axis=1
                    )
    hidden_in = jnp.concatenate([h0[...], h1[...]], axis=0)
    upstream = jnp.concatenate([d0[...], d1[...]], axis=0)
    ysum[...] = jnp.zeros_like(ysum)
    bsum[...] = jnp.zeros_like(bsum)

    def tile(index, carry):
        rows = pl.ds(pl.multiple_of(index * TILE_FF, TILE_FF), TILE_FF)
        up_at = pl.ds(pl.multiple_of(OWN_FF + index * TILE_FF, TILE_FF), TILE_FF)
        gate_rows, up_rows, down_rows = both_w[rows, :], both_w[up_at, :], down_w[rows, :]
        gate = matmul(hidden_in, gate_rows, NT)
        up = matmul(hidden_in, up_rows, NT)
        sigmoid = jax.nn.sigmoid(gate)
        active = gate * sigmoid
        hidden = (active * up).astype(jnp.bfloat16)
        back = matmul(upstream, down_rows, NT)
        gate_back = (back * up * sigmoid * (1.0 + gate * (1.0 - sigmoid))).astype(jnp.bfloat16)
        up_back = (back * active).astype(jnp.bfloat16)
        ysum[...] += matmul(hidden, down_rows, NN)
        bsum[...] += matmul(gate_back, gate_rows, NN) + matmul(up_back, up_rows, NN)
        down_g[rows, :] = matmul(hidden, upstream, TN).astype(jnp.bfloat16)
        both_g[rows, :] = matmul(gate_back, hidden_in, TN).astype(jnp.bfloat16)
        both_g[up_at, :] = matmul(up_back, hidden_in, TN).astype(jnp.bfloat16)
        return carry

    lax.fori_loop(0, OWN_FF // TILE_FF, tile, 0)
    y0[...] = ysum[0:ROWS, :]
    y1[...] = ysum[ROWS:, :].astype(jnp.bfloat16)
    b0[...] = bsum[0:ROWS, :]
    b1[...] = bsum[ROWS:, :].astype(jnp.bfloat16)
    for part, ref in enumerate(grads):
        lanes = pl.ds(pl.multiple_of(order_ref[part] * 256, 256), 256)
        for slot in range(CHIPS):
            row = pl.multiple_of(order_ref[9 + slot] * UNIT, UNIT)
            ref[slot, 0:GRAD_CUT, :] = both_g[pl.ds(row, GRAD_CUT), lanes]
            row = pl.multiple_of(order_ref[25 + slot] * UNIT + GRAD_CUT, 32)
            ref[slot, GRAD_CUT:UNIT, :] = both_g[pl.ds(row, UNIT - GRAD_CUT), lanes]
        for pair in range(8):
            for half in range(2):
                row = pl.multiple_of(order_ref[part] * (2 * UNIT) + 80 * half, 16)
                even = down_g[pl.ds(row, 80), pair * 128 : pair * 128 + 128]
                odd = down_g[pl.ds(row + UNIT, 80), pair * 128 : pair * 128 + 128]
                to = slice(half * 128, half * 128 + 128)
                ref[order_ref[57 + 2 * pair], 160:240, to] = jnp.concatenate([even[:, :64], odd[:, :64]], axis=1)
                ref[order_ref[58 + 2 * pair], 160:240, to] = jnp.concatenate([even[:, 64:], odd[:, 64:]], axis=1)


def feed(order, own_low, other_low, own_up, other_up, weights):
    matrix = ((OWN_FF, WIDE), jnp.bfloat16)
    return call(
        feed_kernel,
        "feed",
        [
            ((ROWS, WIDE), jnp.float32),
            ((ROWS, WIDE), jnp.bfloat16),
            ((ROWS, WIDE), jnp.float32),
            ((ROWS, WIDE), jnp.bfloat16),
        ]
        + [((CHIPS, GRAD_ROWS, 256), jnp.bfloat16)] * 2
        + [((2, CHIPS, GRAD_ROWS, 256), jnp.bfloat16)],
        [((FF, WIDE), jnp.bfloat16), matrix] * 2 + [((2 * ROWS, WIDE), jnp.float32)] * 2,
        (order, own_low, other_low, own_up, other_up, *weights),
        smem=1,
        flops=2 * 9 * 256 * 1024 * 1280,
        moved=22_000_000,
        mib=52,
    )


def norm_back(grad, rows, gain):
    scale = inverse_rms(rows)
    unit = rows * scale
    unit_grad = grad * gain
    mean = jnp.sum(unit_grad * unit, axis=1, keepdims=True) * (1.0 / FEATURES)
    return scale * (unit_grad - unit * mean), jnp.sum(grad * unit, axis=0, keepdims=True)


def middle_back_kernel(
    order_ref, b_ref, more_ref, mid_ref, up_ref, gains_ref, ob_ref, w0, w1, dx_ref, do_ref, dg_ref, grad_ref, whole
):
    load_output(order_ref, (w0, w1), whole)
    back, gain_grad = norm_back(b_ref[...] + more_ref[...].astype(jnp.float32), mid_ref[...], gains_ref[3:4, :])
    dg_ref[...] = gain_grad
    dx = up_ref[...].astype(jnp.float32) + back
    dx_ref[...] = dx
    low = dx.astype(jnp.bfloat16)
    wide = matmul(low, whole[...], NN)
    pieces = [wide[:, part * 256 : part * 256 + 240] for part in range(4)]
    pieces += [jnp.zeros((ROWS, 64), jnp.float32)]
    do_ref[...] = jnp.concatenate(pieces, axis=1).astype(jnp.bfloat16)
    grad_ref[...] = matmul(low, ob_ref[...], TN).astype(jnp.bfloat16)


def middle_backward(order, back, more, middle, upstream, gains, ob, own, other):
    return call(
        middle_back_kernel,
        "middle_backward",
        [
            ((ROWS, WIDE), jnp.float32),
            ((ROWS, WIDE), jnp.bfloat16),
            ((1, WIDE), jnp.float32),
            ((WIDE, WIDE), jnp.bfloat16),
        ],
        [((WIDE, WIDE), jnp.bfloat16)],
        (order, back, more, middle, upstream, gains, ob, own, other),
        smem=1,
        flops=4 * 128 * 1024 * 1024,
        moved=8_000_000,
    )


def project_back_kernel(
    table_ref, x_ref, gains_ref, dx_ref, dg2_ref, dq_ref, dkv0_ref, dkv1_ref, go_ref, cos_ref, sin_ref, *refs
):
    grad_ref = refs[8]
    whole, mixed, low_mixed, gain_tiles = refs[17:]
    load_attend(table_ref, refs[:8], whole)
    cosine, sine = cos_ref[...], sin_ref[...]

    def turn_back(front, back, start):
        mixed[start : start + 32, :] = front * cosine + back * sine
        mixed[start + 32 : start + 64, :] = back * cosine - front * sine

    for head in range(QUERY_HEADS):
        turn_back(dq_ref[head * 64 : head * 64 + 32, :], dq_ref[head * 64 + 32 : head * 64 + 64, :], head * 64)
    for head in range(KEY_VALUE_HEADS):
        ref, at = (dkv0_ref, head) if head < SPLIT else (dkv1_ref, head - SPLIT)
        both = ref[:, at * 128 : at * 128 + 128].astype(jnp.float32).T
        turn_back(both[0:32], both[32:64], 960 + head * 64)
        mixed[1280 + head * 64 : 1344 + head * 64, :] = both[64:]
    mixed[QKV:, :] = jnp.zeros((64, ROWS), jnp.float32)
    keep = lax.broadcasted_iota(jnp.int32, (64, ROWS), 0) < 50
    for owner in range(CTX):
        low_mixed[owner] = jnp.where(keep, mixed[owner * 50 : owner * 50 + 64, :], 0.0).astype(jnp.bfloat16)
    rows = x_ref[...].astype(jnp.float32)
    low = (rows * inverse_rms(rows) * gains_ref[2:3, :]).astype(jnp.bfloat16)
    total = jnp.zeros((ROWS, WIDE), jnp.float32)
    for quarter in range(4):
        left = low_mixed[quarter * 8 : quarter * 8 + 8].reshape(512, ROWS)
        right = whole[quarter * 8 : quarter * 8 + 8].reshape(512, WIDE)
        total = total + matmul(left, right, TN)
    back, gain_grad = norm_back(total, rows, gains_ref[2:3, :])
    grad_ref[...] = dx_ref[...] + back
    row = lax.broadcasted_iota(jnp.int32, (16, 128), 0)
    lane = lax.broadcasted_iota(jnp.int32, (16, 128), 1)
    for owner in range(CTX):
        lanes = slice(owner // 4 * 128, owner // 4 * 128 + 128)
        tile = jnp.where(row == 2, gain_grad[:, lanes], 0.0) + jnp.where(row == 3, dg2_ref[:, lanes], 0.0)
        if owner % 4:
            tile = pltpu.roll(tile, 128 - 32 * (owner % 4), 1)
        gain_tiles[owner] = jnp.where(lane < 32, tile, 0.0)
    for quarter in range(4):
        left = low_mixed[quarter * 8 : quarter * 8 + 8].reshape(512, ROWS)
        whole[quarter * 8 : quarter * 8 + 8] = matmul(left, low, NN).astype(jnp.bfloat16).reshape(8, 64, WIDE)
    for owner in range(CTX):
        whole[owner, 48:64, 0:128] = (whole[owner, 48:64, 0:128].astype(jnp.float32) + gain_tiles[owner]).astype(
            jnp.bfloat16
        )
    for part in range(2):
        for index in range(4):
            for slot in range(8):
                owner = table_ref[part, index * 8 + slot]
                lanes = slice(part * 512, part * 512 + 512)
                ref = refs[9 + 4 * part + index]
                ref[slot, 0:64, :] = whole[owner, :, lanes]
                ref[slot, 64:96, :] = go_ref[pl.ds(pl.multiple_of(owner * 32, 32), 32), lanes]


def project_backward(table, x, gains, dx, dg2, dq, dkv, output_grad, cosine, sine, pieces):
    piece = ((8, 96, 512), jnp.bfloat16)
    return call(
        project_back_kernel,
        "project_backward",
        [((ROWS, WIDE), jnp.float32)] + [piece] * 8,
        [
            ((CTX, 64, WIDE), jnp.bfloat16),
            ((QKV + 64, ROWS), jnp.float32),
            ((CTX, 64, ROWS), jnp.bfloat16),
            ((CTX, 16, 128), jnp.float32),
        ],
        (table, x, gains, dx, dg2, dq, *dkv, output_grad, cosine, sine, *pieces),
        smem=1,
        flops=4 * 2048 * 1024 * 128,
        moved=10_000_000,
    )


def rotary_tables(positions, head_size):
    half_size = head_size // 2
    inverse = jnp.power(10000.0, -2.0 * jnp.arange(half_size, dtype=jnp.float32) / head_size)
    angles = inverse[:, None] * positions.astype(jnp.float32)[None, :]
    return (jnp.cos(angles), jnp.sin(angles))


def adamw(weight, first_old, second_old, gradient, rate, decay):
    first_next = beta_one * first_old + (1.0 - beta_one) * gradient
    second_next = beta_two * second_old + (1.0 - beta_two) * gradient * gradient
    first_hat = first_next / (1.0 - beta_one**STEP)
    second_hat = second_next / (1.0 - beta_two**STEP)
    weight_next = weight - rate * (first_hat / (jnp.sqrt(second_hat) + adam_eps) + decay * weight)
    return (weight_next, first_next, second_next)


def pad_features(rows):
    count = rows.shape[-1] // 30
    shaped = rows.reshape(rows.shape[0], count, 30)
    return jnp.pad(shaped, ((0, 0), (0, 0), (0, 2))).reshape(rows.shape[0], count * 32)


def drop_features(rows):
    count = rows.shape[-1] // 32
    return rows.reshape(rows.shape[0], count, 32)[:, :, :30].reshape(rows.shape[0], count * 30)


def pad_rows(value, count):
    return jnp.pad(value, ((0, count - value.shape[0]), (0, 0)))


def total_of(pieces):
    total = pieces[0].astype(jnp.float32)
    for piece in pieces[1:]:
        total = total + piece.astype(jnp.float32)
    return total


def on_device(
    tokens,
    cotangent,
    blocks,
    attend_weight,
    output_weight,
    gateup_weight,
    down_weight,
    norm_gains,
    attend_first,
    output_first,
    gateup_first,
    down_first,
    gains_first,
    attend_second,
    output_second,
    gateup_second,
    down_second,
    gains_second,
):
    low = jnp.bfloat16
    ctx_index = lax.axis_index("ctx")
    wsh_index = lax.axis_index("wsh")
    core = ctx_index % 2

    attend_shard = pad_features(attend_weight.astype(low).T)
    gain_shard = jnp.pad(norm_gains.astype(low), ((0, 0), (0, 226)))
    attend_shard = pad_rows(jnp.concatenate([attend_shard, gain_shard], axis=0), 64)
    attend_rows = gather_rows(attend_shard, wsh_index)
    down_halves = jnp.pad(down_weight.astype(low), ((0, 0), (0, 2))).reshape(2, 2, UNIT, 32)
    mine = lax.dynamic_index_in_dim(down_halves, core, axis=1, keepdims=False)
    theirs = swap(lax.dynamic_index_in_dim(down_halves, 1 - core, axis=1, keepdims=False), SIBLING)
    upper = core == 1
    joined = jnp.stack([jnp.where(upper, theirs, mine), jnp.where(upper, mine, theirs)], axis=2)
    down_shard = joined.reshape(2, 2, 80, 64).transpose(2, 1, 0, 3).reshape(80, 256)
    gateup_shard = pad_features(gateup_weight.astype(low).T)
    output_shard = jnp.pad(output_weight.astype(low).T, ((0, 2), (0, 16)))
    rest_shard = jnp.concatenate([gateup_shard, output_shard, down_shard], axis=0)
    parts, rest_parts = gather_both(
        [attend_rows[:, :512], attend_rows[:, 512:]], [rest_shard[:REST_CUT], rest_shard[REST_CUT:]]
    )
    attend_pieces = [piece for pair in parts for piece in pair]
    orders = [
        lax.dynamic_index_in_dim(
            jnp.asarray(ROW_ORDER.reshape(8, 4)), (core ^ side) * 4 + wsh_index, axis=0, keepdims=False
        )
        for side in range(2)
    ]
    chips = lax.dynamic_index_in_dim(jnp.asarray(CHIP_ORDER), ctx_index, axis=0, keepdims=False)
    order = jnp.concatenate([*orders, core.reshape(1), chips]).astype(jnp.int32)

    upstream = pad_features(cotangent[0])
    upstream_other = swap(upstream, SIBLING)
    x = after(pad_features(tokens[0]), upstream_other)

    position_index = jnp.arange(2 * CTX, dtype=jnp.int32)
    mine_pair = lax.dynamic_slice_in_dim(blocks, 2 * ctx_index, 2)
    offsets = jnp.arange(BLOCK, dtype=jnp.int32)
    positions = (mine_pair[:, None] * BLOCK + offsets[None, :]).reshape(ROWS)
    cosine, sine = rotary_tables(positions, HEAD_DIMENSION)
    owners = jnp.stack(
        [lax.dynamic_index_in_dim(jnp.asarray(table), ctx_index, axis=0, keepdims=False) for table in ORIGINS]
    )
    slots = owners[:, :, None] * 2 + jnp.arange(2, dtype=jnp.int32)
    held = jnp.sum(
        jnp.where(slots.reshape(2, 64)[:, :, None] == position_index, blocks[None, None, :], 0), axis=2
    )
    lo_slot = (mine_pair[0] > mine_pair[1]).astype(jnp.int32)
    own_blocks = jnp.stack([lo_slot, 1 - lo_slot, jnp.min(mine_pair), jnp.max(mine_pair)])
    meta = jnp.concatenate([own_blocks, held[0], held[1]]).astype(jnp.int32)

    q, keys_first, keys_second, gains = project(owners, x, cosine, sine, attend_pieces)
    rest_joined = join(*after(rest_parts, q))
    rest_parts = zip(rest_joined, swap_all(rest_joined, 3))
    rest_own = jnp.concatenate([jnp.concatenate(pair, axis=0) for pair in rest_parts], axis=1)
    rest_first, rest_second = swap_rows(rest_own, 0), swap_rows(rest_own, 1)
    kv_first, kv_second = gather_chips([keys_first, keys_second])
    rest_third = swap_rows(after(rest_first, kv_first[3], kv_second[3], rest_second), 1)
    attended, attended_turned, log_total = attention_forward(meta, q, [*kv_first, *kv_second])
    rest_pieces = (rest_own, rest_first, rest_second, rest_third)
    output_own = jnp.concatenate([piece[:, 160:192, :] for piece in after(rest_pieces, attended)], axis=2)
    output_other = swap(output_own, SIBLING)
    middle, second_low, attended_wide = middle_forward(
        order, x, attended, gains, output_own, output_other
    )
    second_other = swap(second_low, SIBLING)
    own_y, other_y, own_back, other_back, *rest_grads = feed(
        order, second_low, second_other, upstream, upstream_other, rest_pieces
    )
    back_more = swap(other_back, SIBLING)
    y_more = swap(other_y, SIBLING)
    rest_got = swap_rows(rest_grads[2], 1)
    middle_grad, attended_reverse, gain_second_grad, output_grad = middle_backward(
        order, own_back, back_more, middle, upstream, gains, attended_wide, output_own, output_other
    )
    result = middle + own_y + y_more.astype(jnp.float32)
    layer_output = drop_features(result.astype(low))[None]

    query_grad, *key_value_grads = attention_backward(
        meta, q, attended_reverse, attended_turned, log_total, [*kv_first, *kv_second]
    )
    rest_more = swap_rows(add(rest_grads[1], rest_got[1]), 0)
    kv_grads = scatter_chips(
        [key_value_grads[:4], key_value_grads[4:]], ((), rest_got, ())
    )
    rest_state = []
    for plan, rows in zip(PLANS, (slice(0, GRAD_CUT), slice(GRAD_CUT, GRAD_ROWS))):
        arrays = [array[:, rows, :] for array in (rest_grads[0], rest_got[0], rest_more)]
        kept, sent = [
            total_of([array[half] for array in arrays]).astype(low) for half in (slice(0, 8), slice(8, 16))
        ]
        rest_state.append((kept, swap(sent, plan[3])))
    input_grad, *attend_grads = project_backward(
        owners,
        x,
        gains,
        middle_grad,
        gain_second_grad,
        query_grad,
        kv_grads,
        output_grad,
        cosine,
        sine,
        attend_pieces,
    )
    input_grad = drop_features(input_grad)[None]

    attend_low, attend_high, rest_low, rest_high = scatter_chips(
        [attend_grads[:4], attend_grads[4:]], rest=rest_state
    )
    rest_total = jnp.concatenate([rest_low, rest_high], axis=0).astype(jnp.float32)
    gateup_sum = drop_features(rest_total[0:160]).T
    down_total = rest_total[160:].reshape(80, 2, 2, 2, 32).transpose(2, 1, 0, 3, 4).reshape(2, UNIT, 2, 32)
    down_mine = lax.dynamic_index_in_dim(down_total, core, axis=2, keepdims=False)
    down_theirs = lax.dynamic_index_in_dim(down_total, 1 - core, axis=2, keepdims=False)
    down_got = swap(down_theirs.astype(low), SIBLING).astype(jnp.float32)
    down_sum = jnp.stack([jnp.where(upper, down_got, down_mine), jnp.where(upper, down_mine, down_got)], axis=1)
    down_sum = down_sum.reshape(640, 32)[:, :30]

    attend_rows_sum = jnp.concatenate([attend_low, attend_high], axis=1)
    row_index = jnp.arange(96, dtype=jnp.int32)[:, None]
    attend_parts = scatter_rows(attend_rows_sum, wsh_index, (row_index == 50) | (row_index == 51))
    attend_total = total_of(attend_parts)
    attend_sum = drop_features(attend_total[0:50]).T
    output_total = attend_total[64:94, :240].T
    stacked = jnp.stack([part[50:52, :30] for part in attend_parts]).astype(jnp.float32)
    gains_sum = total_of(
        [lax.dynamic_index_in_dim(stacked, (wsh_index - source) % 4, axis=0, keepdims=False) for source in range(4)]
    )

    output_rate = max(1, QUERY_HEADS * HEAD_DIMENSION * 32 // (CTX * ROWS)) ** (-0.5)
    attend_next = adamw(attend_weight, attend_first, attend_second, attend_sum, 0.02, 0.1)
    output_next = adamw(output_weight, output_first, output_second, output_total, output_rate, 0.1)
    gateup_next = adamw(gateup_weight, gateup_first, gateup_second, gateup_sum, 0.02, 0.1)
    down_next = adamw(down_weight, down_first, down_second, down_sum, 0.02, 0.1)
    gains_next = adamw(norm_gains, gains_first, gains_second, gains_sum, 0.7, 0.0)
    return (layer_output, input_grad, *attend_next, *output_next, *gateup_next, *down_next, *gains_next)


def solution(mesh):
    rows, columns, both = P("wsh", "ctx", None), P(None, "ctx"), P("wsh", "ctx")
    weights = (both, both, both, both, columns)
    return jax.shard_map(
        on_device,
        mesh=mesh,
        in_specs=(rows, rows, P(), *weights, *weights, *weights),
        out_specs=(rows, rows, *([both] * 12), *([columns] * 3)),
        check_vma=False,
    )
```
